256 devices in a mesh: row: 8 (over z_hi, x), col: 32 (over y, z_lo, core).
Axes of the slice: x: 4, y: 4, z: 8 (z_hi: 2, z_lo: 4; z = z_hi * 4 + z_lo), core: 2. Of those that a mesh axis runs over, the one named last changes fastest.
Arguments:
- projector: float32 [18432, 18432], P('row', 'col'), may hold values from -9 to 490, as said below
- saved: float32 [18432, 512], P('col', 'row'), may hold values from -0.0048828125 to 0.0048828125
- grad_slab: float32 [512, 18432], P('col', 'row'), may hold values from -0.03125 to 0.03125
Outputs:
- updated: float32 [18432, 18432], P('row', 'col')
- projected: float32 [512, 18432], P('row', 'col')
The draws below stay inside these ranges and needn't reach their ends.
Inputs may be any that keep to these rules, and one draw needn't show every extreme that they name: projector is symmetric and positive definite, every eigenvalue above 100; its diagonal entries lie between 390 and 490.
All inputs are finite; a program needn't handle non-finite values.
Results may differ from the reference program's by a relative error of at most 0.000071.
Values sent between devices are 32-bit elements; how exact they have to be, the bound alone decides.
A program may use at most 128 MiB of HBM per device.

```python
import jax
import jax.numpy as jnp
from jax import lax

D = 18432
K = 512
R = 512


def draw_projector(key, part):
    base_key = jax.random.fold_in(key, 17)
    entry_key, diag_key = jax.random.split(base_key)
    raw = jax.random.truncated_normal(entry_key, -6.0, 6.0, (D, D), jnp.float32)
    symmetric = (raw + raw.T) * 0.70710678
    lifted = jax.random.uniform(diag_key, (D,), jnp.float32, 400.0, 480.0)
    index = jnp.arange(D)
    return symmetric.at[index, index].add(lifted)


def block_levels(key, shape, cuts, smallest, largest):
    factor_of = 1.0
    for position, parts in cuts:
        heights = jax.random.uniform(jax.random.fold_in(jax.random.fold_in(key, 6), position), (parts,), jnp.float32, smallest / len(cuts), largest / len(cuts))
        factor_of = factor_of * jnp.repeat(jnp.exp(heights), shape[position] // parts).reshape((-1,) + (1,) * (len(shape) - 1 - position))
    return factor_of


def normal_values(key, extent, scale, bound, shards=(), held_as=jnp.bfloat16):
    array = scale * jax.random.normal(key, extent, jnp.float32)
    if shards:
        array = array * block_levels(key, extent, shards, -0.22, 0.18)
    return jnp.clip(array, -bound, bound).astype(held_as)


def setup_inputs(seed: int = 0) -> dict:
    key_of = jax.random.split(jax.random.key(seed), 4)
    return {
        "projector": draw_projector(jax.random.fold_in(key_of[3], 71), 0),
        "saved": normal_values(key_of[1], (D, K), (1.0 / (21 * D ** 0.5)), 0.0048828125, ((0, 32), (1, 8)), jnp.float32),
        "grad_slab": normal_values(key_of[2], (R, D), 0.002, 0.03125, ((0, 32), (1, 8)), jnp.float32),
    }


def reference(projector, saved, grad_slab):
    highest = lax.Precision.HIGHEST
    y_all = jnp.dot(projector.astype(jnp.float32), saved.astype(jnp.float32), precision=highest, preferred_element_type=jnp.float32)
    system = jnp.eye(K, dtype=jnp.float32) + jnp.dot(saved.T.astype(jnp.float32), y_all.astype(jnp.float32), precision=highest, preferred_element_type=jnp.float32)
    factor = jnp.linalg.cholesky(system)
    solved = jax.scipy.linalg.cho_solve((factor, True), y_all.T)
    blocks = projector.reshape(8, D // 8, D)
    y_blocks = y_all.reshape(8, D // 8, K)
    g_blocks = grad_slab.reshape(R, 8, D // 8).transpose(1, 0, 2)

    def one_block(inputs):
        p_block, y_block, g_block = inputs
        new_block = p_block - jnp.dot(y_block.astype(jnp.float32), solved.astype(jnp.float32), precision=highest, preferred_element_type=jnp.float32)
        return (new_block, jnp.dot(g_block.astype(jnp.float32), new_block.astype(jnp.float32), precision=highest, preferred_element_type=jnp.float32))
    new_blocks, contribs = lax.map(one_block, (blocks, y_blocks, g_blocks))
    return (new_blocks.reshape(D, D), jnp.sum(contribs, axis=0))
```

```python
import functools

import jax
import jax.numpy as jnp
from jax import lax
from jax.experimental import pallas as pl
from jax.experimental.pallas import tpu as pltpu
from jax.sharding import PartitionSpec as P

MESH = pl.DeviceIdType.MESH
F32 = jnp.float32
BF16 = jnp.bfloat16
NN = (((1,), (0,)), ((), ()))
NT = (((1,), (1,)), ((), ()))
TN = (((0,), (0,)), ((), ()))


def split(x):
    hi = x.astype(BF16)
    return hi, (x - hi.astype(F32)).astype(BF16)


def dot3(a_hi, a_lo, b_hi, b_lo, dims=NN):
    dot = functools.partial(lax.dot_general, dimension_numbers=dims, preferred_element_type=F32)
    return dot(a_hi, b_hi) + (dot(a_hi, b_lo) + dot(a_lo, b_hi))


def dot_full(a, b, dims=NN):
    return lax.dot_general(a, b, dims, precision=lax.Precision.HIGHEST, preferred_element_type=F32)


class Place:
    def __init__(self):
        self.row = lax.axis_index("row")
        self.col = lax.axis_index("col")
        self.zh = self.row // 4
        self.x = self.row % 4
        self.y = self.col // 8
        self.zl = (self.col // 2) % 4
        self.k = self.col % 2

    def at(self, zh=None, x=None, y=None, zl=None, k=None):
        zh = self.zh if zh is None else zh
        x = self.x if x is None else x
        y = self.y if y is None else y
        zl = self.zl if zl is None else zl
        k = self.k if k is None else k
        return (zh * 4 + x, y * 8 + zl * 2 + k)

    def sib(self):
        return self.at(k=1 - self.k)

    def anti(self):
        return self.at(zh=1 - self.zh)

    def xd(self, d):
        return self.at(x=(self.x + d) % 4)

    def yd(self, d):
        return self.at(y=(self.y + d) % 4)

    def zd(self, d):
        return self.at(zl=(self.zl + d) % 4)

    def strip(self, q):
        return (self.col // 4, 8 * (self.col % 4) + q)

    def strip_source(self, r):
        return (r, 4 * self.row + self.col // 8)

    def is_me(self, dev):
        return jnp.logical_and(dev[0] == self.row, dev[1] == self.col)


class Links:
    def __init__(self, me, send, recv):
        self.me, self.send, self.recv, self.used = me, send, recv, 0
        self.sent = []

    def slot(self, n=1):
        self.used += n
        assert self.used <= NSEM, self.used
        return self.used - n

    def push(self, src, dst, dev):
        i = self.slot()
        copy = pltpu.make_async_remote_copy(
            src_ref=src, dst_ref=dst, send_sem=self.send.at[i], recv_sem=self.recv.at[i],
            device_id=dev, device_id_type=MESH)
        copy.start()
        self.sent.append(copy)
        return copy

    def finish(self):
        for copy in self.sent:
            copy.wait_send()


NSEM = 160


class PlaneGather:
    def __init__(self, links, buf):
        self.links, self.buf, self.me = links, buf, links.me

    def start(self):
        me, buf = self.me, self.buf
        mine = buf.at[me.y, me.zl, me.k]
        self.z = [self.links.push(mine, mine, me.zd(d)) for d in (1, 2, 3)]

    def pair(self, y):
        part = self.buf.at[y, :, self.me.k]
        self.pairs.append(self.links.push(part, part, self.me.sib()))

    def step1(self):
        me, buf = self.me, self.buf
        self.pairs = []
        for copy in self.z:
            copy.wait_recv()
        mine = buf.at[me.y, :, me.k]
        self.up = self.links.push(mine, mine, me.yd(1))
        self.down = self.links.push(mine, mine, me.yd(3))
        self.pair(me.y)

    def step2(self):
        me, buf = self.me, self.buf
        below, above = (me.y + 3) % 4, (me.y + 1) % 4
        self.up.wait_recv()
        half = buf.at[below, pl.ds(0, 2), me.k]
        self.up2 = self.links.push(half, half, me.yd(1))
        self.down.wait_recv()
        half = buf.at[above, pl.ds(2, 2), me.k]
        self.down2 = self.links.push(half, half, me.yd(3))
        self.pair(below)
        self.pair(above)

    def step3(self):
        self.up2.wait_recv()
        self.down2.wait_recv()
        self.pair((self.me.y + 2) % 4)

    def finish(self):
        for copy in self.pairs:
            copy.wait_recv()


class RowGather:
    def __init__(self, links, buf):
        self.links, self.buf, self.me = links, buf, links.me

    def start(self):
        me = self.me
        mine = self.buf.at[me.row]
        self.far = self.links.push(mine, mine, me.anti())
        self.near = [self.links.push(mine, mine, me.xd(d)) for d in (1, 2, 3)]

    def step(self):
        me = self.me
        self.far.wait_recv()
        other = self.buf.at[(me.row + 4) % 8]
        self.near2 = [self.links.push(other, other, me.xd(d)) for d in (1, 2, 3)]

    def finish(self):
        for copy in self.near + self.near2:
            copy.wait_recv()


def barrier(me):
    sem = pltpu.get_barrier_semaphore()
    devs = [me.sib(), me.anti()]
    devs += [f(d) for f in (me.xd, me.yd, me.zd) for d in (1, 2, 3)]
    for dev in devs:
        pl.semaphore_signal(sem, inc=1, device_id=dev, device_id_type=MESH)
    for dev in [me.strip_source(r) for r in range(8)] + [me.strip(me.row)]:

        @pl.when(jnp.logical_not(me.is_me(dev)))
        def _():
            pl.semaphore_signal(sem, inc=1, device_id=dev, device_id_type=MESH)

    count = jnp.int32(len(devs))
    for dev in [me.strip(q) for q in range(8)] + [me.strip_source(me.col % 8)]:
        count += jnp.where(me.is_me(dev), 0, 1)
    pl.semaphore_wait(sem, count)


class LooseCopy:
    def __init__(self, links, src, dst, dev, send, recv):
        me = links.me
        self.remote = pltpu.make_async_remote_copy(
            src_ref=src, dst_ref=dst, send_sem=links.send.at[send], recv_sem=links.recv.at[recv],
            device_id=dev, device_id_type=MESH)
        self.here = me.is_me(dev)
        self.local = pltpu.make_async_copy(src, dst, links.recv.at[recv])
        pl.when(jnp.logical_not(self.here))(lambda: self.remote.start())
        pl.when(self.here)(lambda: self.local.start())
        links.sent.append(self)

    def wait_send(self):
        pl.when(jnp.logical_not(self.here))(lambda: self.remote.wait_send())


def invert(a):
    n = a.shape[0]
    ri = lax.broadcasted_iota(jnp.int32, (n, n), 0)
    ci = lax.broadcasted_iota(jnp.int32, (n, n), 1)
    for k in range(n):
        row = a[k:k + 1, :]
        col = a[:, k:k + 1]
        p = 1.0 / a[k:k + 1, k:k + 1]
        rp = row * p
        b = jnp.where(ci == k, -(col * p), a - col * rp)
        a = jnp.where(ri == k, jnp.where(ci[0:1] == k, p, rp), b)
    return a


def mega(p_hbm, xp_ref, g_ref, yr_hbm, wt_ref, proj_ref,
         pst, p_hi, p_lo, xbuf, xs, xc_hi, xc_lo, gbuf, part, d2d, csum, r1, r2, rz, ybuf, ycb, x72,
         gram, gram_in, ga, gy_in, gb, gx_in, gc, gz_in, gout, amat, gpp, gpx, gps, gpa, gp64,
         gyp, gyd, gya, gyy, gyb, gyz, gyo, send, recv, lsem):
    me = Place()
    row, col, zh, x, y, zl, k = me.row, me.col, me.zh, me.x, me.y, me.zl, me.k
    links = Links(me, send, recv)
    pcopy = pltpu.make_async_copy(p_hbm, pst, lsem.at[0])
    pcopy.start()
    xbuf[row] = xp_ref[...]
    gbuf[y, zl, k] = g_ref[...]
    barrier(me)
    xg = RowGather(links, xbuf)
    xg.start()
    base_s, base_r = links.slot(8), links.slot(8)
    for q in range(8):
        LooseCopy(links, xp_ref.at[pl.ds(72 * (q % 4), 72)], xs.at[row], me.strip(q), base_s + q, base_r + row)
    gg = PlaneGather(links, gbuf)
    gg.start()
    pcopy.wait()

    @pl.loop(0, 36)
    def _(i):
        rows = pl.ds(pl.multiple_of(i * 64, 64), 64)
        p_hi[rows], p_lo[rows] = split(pst[rows])

    xg.step()
    gg.step1()
    lane = lax.broadcasted_iota(jnp.int32, (288, 128), 1)
    xg.finish()
    for m in range(4):
        b0, b1 = xbuf[2 * m], xbuf[2 * m + 1]
        cols = pl.ds(128 * m, 128)
        xc_hi[0:288, cols], xc_lo[0:288, cols] = split(jnp.where(lane < 64, b0, pltpu.roll(b1, 64, 1)))
        xc_hi[288:576, cols], xc_lo[288:576, cols] = split(jnp.where(lane < 64, pltpu.roll(b0, 64, 1), b1))

    def multiply(ay):
        @pl.loop(0, 4)
        def _(z):
            rows = pl.ds(pl.multiple_of(ay * 576 + z * 144, 144), 144)
            part[ay, z] = dot3(p_hi[rows], p_lo[rows], xc_hi[...], xc_lo[...]).reshape(2, 72, 512)
        return links.push(part.at[ay, :, 1 - k], d2d.at[ay], me.sib())

    def add_pair(ay, copy):
        copy.wait_recv()

        @pl.loop(0, 4)
        def _(z):
            csum[ay, z] = part[ay, z, k] + d2d[ay, z]

    y1, y2, y3 = (y + 1) % 4, (y + 2) % 4, (y + 3) % 4
    c2 = multiply(y2)
    c1 = multiply(y1)
    add_pair(y2, c2)
    up = links.push(csum.at[y2, pl.ds(0, 2)], r1.at[0], me.yd(1))
    down = links.push(csum.at[y2, pl.ds(2, 2)], r1.at[1], me.yd(3))
    c3 = multiply(y3)
    add_pair(y1, c1)
    c0 = multiply(y)
    add_pair(y3, c3)
    up.wait_recv()
    for z in range(2):
        csum[y1, z] += r1[0, z]
    up2 = links.push(csum.at[y1], r2.at[0], me.yd(1))
    down.wait_recv()
    for z in range(2):
        csum[y3, z + 2] += r1[1, z]
    down2 = links.push(csum.at[y3], r2.at[1], me.yd(3))
    add_pair(y, c0)

    for r in range(8):
        links_recv = pltpu.make_async_copy(xs.at[r], xs.at[r], recv.at[base_r + r])
        links_recv.wait()
    lane72 = lax.broadcasted_iota(jnp.int32, (72, 128), 1)
    flip = (col % 8) >= 4
    for m in range(4):
        b0, b1 = xs[2 * m], xs[2 * m + 1]
        first = jnp.where(lane72 < 64, b0, pltpu.roll(b1, 64, 1))
        second = jnp.where(lane72 < 64, pltpu.roll(b0, 64, 1), b1)
        x72[:, 128 * m:128 * m + 128] = jnp.where(flip, second, first)

    gg.step2()
    up2.wait_recv()
    down2.wait_recv()

    @pl.loop(0, 4)
    def _(z):
        csum[y, z] = csum[y, z] + (r2[0, z] + r2[1, z])

    zc = []
    for d in (1, 2, 3):
        zc.append(links.push(csum.at[y, (zl + d) % 4], rz.at[d - 1], me.zd(d)))
    gg.step3()
    for copy in zc:
        copy.wait_recv()
    y72 = csum[y, zl] + rz[0] + (rz[1] + rz[2])
    ybuf[y, zl, k] = y72
    yg = PlaneGather(links, ybuf)
    yg.start()
    yc = LooseCopy(links, ybuf.at[y, zl, k], ycb.at[col % 8], me.strip_source(col % 8), links.slot(), links.slot())

    yv = ybuf[y, zl, k]
    for i, (top, left) in enumerate(((0, 0), (128, 0), (128, 256), (0, 128))):
        g = dot_full(x72[:, 128 * i:128 * i + 128], yv[:, :128 * i + 128], TN)
        gram[top // 128, :, :, :, left:left + 128 * i + 128] = g.reshape(4, 4, 8, 128 * i + 128)
    copy = links.push(gram.at[1 - k], gram_in, me.sib())
    copy.wait_recv()
    for i in range(4):
        ga[i] = gram[k, i] + gram_in[i]
    cs = [links.push(ga.at[(y + d) % 4], gy_in.at[d - 1], me.yd(d)) for d in (1, 2, 3)]
    for copy in cs:
        copy.wait_recv()
    gb[...] = ga[y] + gy_in[0] + (gy_in[1] + gy_in[2])
    cs = [links.push(gb.at[(x + d) % 4], gx_in.at[d - 1], me.xd(d)) for d in (1, 2, 3)]
    for copy in cs:
        copy.wait_recv()
    gc[0] = gb[x] + gx_in[0] + (gx_in[1] + gx_in[2])
    cs = [links.push(gc.at[0], gz_in.at[d - 1], me.zd(d)) for d in (1, 2, 3)]
    for copy in cs:
        copy.wait_recv()
    gc[1] = gc[0] + gz_in[0] + (gz_in[1] + gz_in[2])
    copy = links.push(gc.at[1], gz_in.at[3], me.anti())
    copy.wait_recv()
    gout[k, y, x] = gc[1] + gz_in[3]
    cs = [links.push(gout.at[k, y, x], gout.at[k, y, x], me.xd(d)) for d in (1, 2, 3)]
    for copy in cs:
        copy.wait_recv()
    cs = [links.push(gout.at[k, y], gout.at[k, y], me.yd(d)) for d in (1, 2, 3)]
    for copy in cs:
        copy.wait_recv()
    copy = links.push(gout.at[k], gout.at[k], me.sib())
    yg.step1()
    yc.remote.wait_recv()
    ycg = RowGather(links, ycb)
    ycg.start()
    copy.wait_recv()

    ri = lax.broadcasted_iota(jnp.int32, (128, 128), 0)
    ci = lax.broadcasted_iota(jnp.int32, (128, 128), 1)
    for i, (top, left) in enumerate(((0, 0), (1, 0), (1, 256), (0, 128))):
        for j in range(i + 1):
            b = gout[top, :, :, :, left + 128 * j:left + 128 * j + 128].reshape(128, 128)
            if i == j:
                amat[128 * i:128 * i + 128, 128 * i:128 * i + 128] = b + jnp.where(ri == ci, 1.0, 0.0)
            else:
                amat[128 * i:128 * i + 128, 128 * j:128 * j + 128] = b
                amat[128 * j:128 * j + 128, 128 * i:128 * i + 128] = b.T

    def eliminate(j):
        at = pl.ds(pl.multiple_of(j * 128, 128), 128)
        inv = invert(amat[at, at])
        c = amat[:, at]
        r = dot_full(inv, amat[at, :])
        amat[...] -= dot_full(c, r)
        amat[:, at] = -dot_full(c, inv)
        amat[at, :] = r
        amat[at, at] = inv

    def gp_multiply(i):
        rows = pl.ds(pl.multiple_of(i * 64, 64), 64)
        ys, zs = i // 2, (i % 2) * 2
        g = gbuf[ys, pl.ds(zs, 2)].reshape(64, 2304)
        g_hi, g_lo = split(g)
        gpp[i % 4, i // 4] = dot3(g_hi, g_lo, p_hi[...], p_lo[...])

    gg.finish()

    @pl.loop(0, 8)
    def _(i):
        gp_multiply(i)

    cs = [links.push(gpp.at[(x + d) % 4], gpx.at[d - 1], me.xd(d)) for d in (1, 2, 3)]
    ycg.step()
    pl.loop(0, 2)(eliminate)
    yg.step2()
    for copy in cs:
        copy.wait_recv()
    gps[...] = gpp[x] + gpx[0] + (gpx[1] + gpx[2])
    gcopy = links.push(gps.at[1 - zh], gpa, me.anti())
    pl.loop(2, 3)(eliminate)
    yg.step3()
    gcopy.wait_recv()
    gp64[...] = gps[zh] + gpa[...]
    gp_hi, gp_lo = split(gp64[...])
    gyp[...] = dot3(gp_hi, gp_lo, xc_hi[...], xc_lo[...]).reshape(2, 4, 8, 512)
    copy = links.push(gyp.at[1 - k], gyd, me.sib())
    copy.wait_recv()
    gya[...] = gyp[k] + gyd[...]
    cs = [links.push(gya.at[(y + d) % 4], gyy.at[d - 1], me.yd(d)) for d in (1, 2, 3)]
    for copy in cs:
        copy.wait_recv()
    gyb[...] = gya[y] + gyy[0] + (gyy[1] + gyy[2])
    cs = [links.push(gyb, gyz.at[d - 1], me.zd(d)) for d in (1, 2, 3)]
    for copy in cs:
        copy.wait_recv()
    gyo[k, y] = gyb[...] + gyz[0] + (gyz[1] + gyz[2])
    cs = [links.push(gyo.at[k, y], gyo.at[k, y], me.yd(d)) for d in (1, 2, 3)]
    for copy in cs:
        copy.wait_recv()
    gycopy = links.push(gyo.at[k], gyo.at[k], me.sib())
    pl.loop(3, 4)(eliminate)
    yg.finish()
    out = pltpu.make_async_copy(ybuf, yr_hbm, lsem.at[1])
    out.start()
    ycg.finish()
    s_hi, s_lo = split(amat[...])

    @pl.loop(0, 4)
    def _(i):
        b_hi, b_lo = split(ycb[pl.ds(i * 2, 2)].reshape(144, 512))
        wt_ref[pl.ds(pl.multiple_of(i * 144, 144), 144), :] = dot3(b_hi, b_lo, s_hi, s_lo)

    gycopy.wait_recv()
    gy_hi, gy_lo = split(gyo[...].reshape(64, 512))
    w_hi, w_lo = split(wt_ref[...])
    proj_ref[...] = gp64[...] - dot3(gy_hi, gy_lo, w_hi, w_lo, NT)
    out.wait()
    links.finish()


def mega_call(projector, packed, grad):
    vm = lambda *shape, dtype=F32: pltpu.VMEM(shape, dtype)
    scratch = [
        vm(2304, 576), vm(2304, 576, dtype=BF16), vm(2304, 576, dtype=BF16),
        vm(8, 288, 128), vm(8, 72, 128), vm(576, 512, dtype=BF16), vm(576, 512, dtype=BF16),
        vm(4, 4, 2, 16, 2304), vm(4, 4, 2, 72, 512), vm(4, 4, 72, 512), vm(4, 4, 72, 512),
        vm(2, 2, 72, 512), vm(2, 4, 72, 512), vm(3, 72, 512),
        vm(4, 4, 2, 72, 512), vm(8, 72, 512), vm(72, 512),
        vm(2, 4, 4, 8, 640), vm(4, 4, 8, 640), vm(4, 4, 8, 640), vm(3, 4, 8, 640),
        vm(4, 8, 640), vm(3, 8, 640), vm(2, 8, 640), vm(4, 8, 640), vm(2, 4, 4, 8, 640), vm(512, 512),
        vm(4, 2, 64, 576), vm(3, 2, 64, 576), vm(2, 64, 576), vm(64, 576), vm(64, 576),
        vm(2, 4, 8, 512), vm(4, 8, 512), vm(4, 8, 512), vm(3, 8, 512), vm(8, 512), vm(3, 8, 512), vm(2, 4, 8, 512),
        pltpu.SemaphoreType.DMA((NSEM,)), pltpu.SemaphoreType.DMA((NSEM,)), pltpu.SemaphoreType.DMA((2,)),
    ]
    anyspace = pl.BlockSpec(memory_space=pl.ANY)
    vmem = pl.BlockSpec(memory_space=pltpu.VMEM)
    return pl.pallas_call(
        mega,
        out_shape=[
            jax.ShapeDtypeStruct((4, 4, 2, 72, 512), F32),
            jax.ShapeDtypeStruct((576, 512), F32),
            jax.ShapeDtypeStruct((64, 576), F32),
        ],
        in_specs=[anyspace, vmem, vmem],
        out_specs=[anyspace, vmem, vmem],
        scratch_shapes=scratch,
        compiler_params=pltpu.CompilerParams(
            collective_id=0, has_side_effects=True, vmem_limit_bytes=58 * 1024 * 1024),
        name="solve",
    )(projector, packed, grad)


def update_kernel(p_ref, y_ref, wt_ref, o_ref, w_hi, w_lo):
    @pl.when(pl.program_id(0) == 0)
    def _():
        w_hi[...], w_lo[...] = split(wt_ref[...])

    y_hi, y_lo = split(y_ref[...])
    o_ref[...] = p_ref[...] - dot3(y_hi, y_lo, w_hi[...], w_lo[...], NT)


def update_call(projector, y_rows, wt):
    block = 256
    return pl.pallas_call(
        update_kernel,
        grid=(2304 // block,),
        out_shape=jax.ShapeDtypeStruct((2304, 576), F32),
        in_specs=[
            pl.BlockSpec((block, 576), lambda i: (i, 0)),
            pl.BlockSpec((block, 512), lambda i: (i, 0)),
            pl.BlockSpec((576, 512), lambda i: (0, 0)),
        ],
        out_specs=pl.BlockSpec((block, 576), lambda i: (i, 0)),
        scratch_shapes=[pltpu.VMEM((576, 512), BF16), pltpu.VMEM((576, 512), BF16)],
        compiler_params=pltpu.CompilerParams(vmem_limit_bytes=32 * 1024 * 1024),
        name="update",
    )(projector, y_rows, wt)


def local(projector, saved, grad_slab):
    packed = jnp.concatenate([saved[:288], saved[288:]], axis=1)
    y_rows, wt, projected = mega_call(projector, packed, grad_slab)
    updated = update_call(projector, y_rows.reshape(2304, 512), wt)
    return (updated, projected)


def solution(mesh):
    return jax.shard_map(
        local,
        mesh=mesh,
        in_specs=(P("row", "col"), P("col", "row"), P("col", "row")),
        out_specs=(P("row", "col"), P("row", "col")),
        check_vma=False,
    )
```

```python
import functools

import jax
import jax.numpy as jnp
from jax import lax
from jax.experimental import pallas as pl
from jax.experimental.pallas import tpu as pltpu
from jax.sharding import PartitionSpec as P

MESH = pl.DeviceIdType.MESH
F32 = jnp.float32
BF16 = jnp.bfloat16
NN = (((1,), (0,)), ((), ()))
NT = (((1,), (1,)), ((), ()))
TN = (((0,), (0,)), ((), ()))


def split(x):
    hi = x.astype(BF16)
    return hi, (x - hi.astype(F32)).astype(BF16)


def dot3(a_hi, a_lo, b_hi, b_lo, dims=NN):
    dot = functools.partial(lax.dot_general, dimension_numbers=dims, preferred_element_type=F32)
    return dot(a_hi, b_hi) + (dot(a_hi, b_lo) + dot(a_lo, b_hi))


def dot_full(a, b, dims=NN):
    return lax.dot_general(a, b, dims, precision=lax.Precision.HIGHEST, preferred_element_type=F32)


class Place:
    def __init__(self):
        self.row = lax.axis_index("row")
        self.col = lax.axis_index("col")
        self.zh = self.row // 4
        self.x = self.row % 4
        self.y = self.col // 8
        self.zl = (self.col // 2) % 4
        self.k = self.col % 2

    def at(self, zh=None, x=None, y=None, zl=None, k=None):
        zh = self.zh if zh is None else zh
        x = self.x if x is None else x
        y = self.y if y is None else y
        zl = self.zl if zl is None else zl
        k = self.k if k is None else k
        return (zh * 4 + x, y * 8 + zl * 2 + k)

    def sib(self):
        return self.at(k=1 - self.k)

    def anti(self):
        return self.at(zh=1 - self.zh)

    def xd(self, d):
        return self.at(x=(self.x + d) % 4)

    def yd(self, d):
        return self.at(y=(self.y + d) % 4)

    def zd(self, d):
        return self.at(zl=(self.zl + d) % 4)

    def strip(self, q):
        return (self.col // 4, 8 * (self.col % 4) + q)

    def strip_source(self, r):
        return (r, 4 * self.row + self.col // 8)

    def is_me(self, dev):
        return jnp.logical_and(dev[0] == self.row, dev[1] == self.col)


class Links:
    def __init__(self, me, send, recv):
        self.me, self.send, self.recv, self.used = me, send, recv, 0
        self.sent = []

    def slot(self, n=1):
        self.used += n
        assert self.used <= NSEM, self.used
        return self.used - n

    def push(self, src, dst, dev):
        i = self.slot()
        copy = pltpu.make_async_remote_copy(
            src_ref=src, dst_ref=dst, send_sem=self.send.at[i], recv_sem=self.recv.at[i],
            device_id=dev, device_id_type=MESH)
        copy.start()
        self.sent.append(copy)
        return copy

    def finish(self):
        for copy in self.sent:
            copy.wait_send()


NSEM = 160


class PlaneGather:
    def __init__(self, links, buf):
        self.links, self.buf, self.me = links, buf, links.me

    def start(self):
        me, buf = self.me, self.buf
        mine = buf.at[me.y, me.zl, me.k]
        self.z = [self.links.push(mine, mine, me.zd(d)) for d in (1, 2, 3)]

    def pair(self, y):
        part = self.buf.at[y, :, self.me.k]
        self.pairs.append(self.links.push(part, part, self.me.sib()))

    def step1(self):
        me, buf = self.me, self.buf
        self.pairs = []
        for copy in self.z:
            copy.wait_recv()
        mine = buf.at[me.y, :, me.k]
        self.up = self.links.push(mine, mine, me.yd(1))
        self.down = self.links.push(mine, mine, me.yd(3))
        self.pair(me.y)

    def step2(self):
        me, buf = self.me, self.buf
        below, above = (me.y + 3) % 4, (me.y + 1) % 4
        self.up.wait_recv()
        half = buf.at[below, pl.ds(0, 2), me.k]
        self.up2 = self.links.push(half, half, me.yd(1))
        self.down.wait_recv()
        half = buf.at[above, pl.ds(2, 2), me.k]
        self.down2 = self.links.push(half, half, me.yd(3))
        self.pair(below)
        self.pair(above)

    def step3(self):
        self.up2.wait_recv()
        self.down2.wait_recv()
        self.pair((self.me.y + 2) % 4)

    def finish(self):
        for copy in self.pairs:
            copy.wait_recv()


class RowGather:
    def __init__(self, links, buf):
        self.links, self.buf, self.me = links, buf, links.me

    def start(self):
        me = self.me
        mine = self.buf.at[me.row]
        self.far = self.links.push(mine, mine, me.anti())
        self.near = [self.links.push(mine, mine, me.xd(d)) for d in (1, 2, 3)]

    def step(self):
        me = self.me
        self.far.wait_recv()
        other = self.buf.at[(me.row + 4) % 8]
        self.near2 = [self.links.push(other, other, me.xd(d)) for d in (1, 2, 3)]

    def finish(self):
        for copy in self.near + self.near2:
            copy.wait_recv()


def barrier(me):
    sem = pltpu.get_barrier_semaphore()
    devs = [me.sib(), me.anti()]
    devs += [f(d) for f in (me.xd, me.yd, me.zd) for d in (1, 2, 3)]
    for dev in devs:
        pl.semaphore_signal(sem, inc=1, device_id=dev, device_id_type=MESH)
    for dev in [me.strip_source(r) for r in range(8)] + [me.strip(me.row)]:

        @pl.when(jnp.logical_not(me.is_me(dev)))
        def _():
            pl.semaphore_signal(sem, inc=1, device_id=dev, device_id_type=MESH)

    count = jnp.int32(len(devs))
    for dev in [me.strip(q) for q in range(8)] + [me.strip_source(me.col % 8)]:
        count += jnp.where(me.is_me(dev), 0, 1)
    pl.semaphore_wait(sem, count)


class LooseCopy:
    def __init__(self, links, src, dst, dev, send, recv):
        me = links.me
        self.remote = pltpu.make_async_remote_copy(
            src_ref=src, dst_ref=dst, send_sem=links.send.at[send], recv_sem=links.recv.at[recv],
            device_id=dev, device_id_type=MESH)
        self.here = me.is_me(dev)
        self.local = pltpu.make_async_copy(src, dst, links.recv.at[recv])
        pl.when(jnp.logical_not(self.here))(lambda: self.remote.start())
        pl.when(self.here)(lambda: self.local.start())
        links.sent.append(self)

    def wait_send(self):
        pl.when(jnp.logical_not(self.here))(lambda: self.remote.wait_send())


def lanes(v, j):
    return jnp.broadcast_to(v[:, j:j + 1], (8, 128))


def rows8(v, i):
    return jnp.broadcast_to(v[i:i + 1, :], (8, 128))


def total(terms):
    while len(terms) > 1:
        terms = [a + b for a, b in zip(terms[::2], terms[1::2])]
    return terms[0]


def invert(a):
    s = lax.broadcasted_iota(jnp.int32, (8, 128), 0)
    lane = lax.broadcasted_iota(jnp.int32, (8, 128), 1)
    tiles = [a[8 * i:8 * i + 8, :] for i in range(16)]
    for g in range(16):
        e = [lanes(tiles[g], 8 * g + j) for j in range(8)]
        for i in range(8):
            p = 1.0 / rows8(e[i], i)
            new = []
            for j in range(8):
                if j == i:
                    new.append(jnp.where(s == i, p, -(e[i] * p)))
                else:
                    r = rows8(e[j], i) * p
                    new.append(jnp.where(s == i, r, e[j] - e[i] * r))
            e = new
        inside = jnp.logical_and(lane >= 8 * g, lane < 8 * g + 8)
        unit = jnp.where(inside, jnp.where(lane - 8 * g == s, 1.0, 0.0), tiles[g])
        pivot = total([e[j] * rows8(unit, j) for j in range(8)])
        each = [rows8(pivot, j) for j in range(8)]
        tiles = [
            pivot if i == g else jnp.where(inside, 0.0, t) - total([lanes(t, 8 * g + j) * each[j] for j in range(8)])
            for i, t in enumerate(tiles)
        ]
    return jnp.concatenate(tiles, axis=0)


def mega(p_hbm, xt_ref, g_ref, yr_hbm, wt_ref, proj_ref,
         pst, p_hi, p_lo, xbuf, xs, xc_hi, xc_lo, gbuf, part, d2d, csum, r1, r2, rz, ybuf, ycb, x72,
         gram, gram_in, ga, gy_in, gb, gx_in, gc, gz_in, gout, amat, gpp, gpx, gps, gpa, gp64,
         gyp, gyd, gya, gyy, gyb, gyz, gyo, send, recv, lsem):
    me = Place()
    row, col, zh, x, y, zl, k = me.row, me.col, me.zh, me.x, me.y, me.zl, me.k
    links = Links(me, send, recv)
    pcopy = pltpu.make_async_copy(p_hbm, pst, lsem.at[0])
    pcopy.start()
    xp_ref = xbuf.at[row]
    xp_ref[...] = jnp.concatenate([xt_ref[:, 0:288], xt_ref[:, 288:576]], axis=0).T
    gbuf[y, zl, k] = g_ref[...]
    barrier(me)
    xg = RowGather(links, xbuf)
    xg.start()
    gg = PlaneGather(links, gbuf)
    gg.start()
    pcopy.wait()

    @pl.loop(0, 18)
    def _(i):
        rows = pl.ds(pl.multiple_of(i * 128, 128), 128)
        p_hi[rows], p_lo[rows] = split(pst[:, rows].T)

    xg.step()
    gg.step1()
    lane = lax.broadcasted_iota(jnp.int32, (288, 128), 1)
    xg.finish()
    base_s, base_r = links.slot(8), links.slot(8)
    for q in range(8):
        LooseCopy(links, xp_ref.at[pl.ds(72 * (q % 4), 72)], xs.at[row], me.strip(q), base_s + q, base_r + row)
    for m in range(4):
        b0, b1 = xbuf[2 * m], xbuf[2 * m + 1]
        cols = pl.ds(128 * m, 128)
        xc_hi[0:288, cols], xc_lo[0:288, cols] = split(jnp.where(lane < 64, b0, pltpu.roll(b1, 64, 1)))
        xc_hi[288:576, cols], xc_lo[288:576, cols] = split(jnp.where(lane < 64, pltpu.roll(b0, 64, 1), b1))

    def multiply(ay):
        @pl.loop(0, 2)
        def _(z):
            rows = pl.ds(pl.multiple_of(ay * 576 + z * 288, 288), 288)
            part[ay, pl.ds(z * 2, 2)] = dot3(p_hi[rows], p_lo[rows], xc_hi[...], xc_lo[...]).reshape(2, 2, 72, 512)

        return links.push(part.at[ay, :, 1 - k], d2d.at[ay], me.sib())

    def add_pair(ay, copy):
        copy.wait_recv()

        @pl.loop(0, 4)
        def _(z):
            csum[ay, z] = part[ay, z, k] + d2d[ay, z]

    y1, y2, y3 = (y + 1) % 4, (y + 2) % 4, (y + 3) % 4
    c2 = multiply(y2)
    c1 = multiply(y1)
    add_pair(y2, c2)
    up = links.push(csum.at[y2, pl.ds(0, 2)], r1.at[0], me.yd(1))
    down = links.push(csum.at[y2, pl.ds(2, 2)], r1.at[1], me.yd(3))
    c3 = multiply(y3)
    add_pair(y1, c1)
    c0 = multiply(y)
    add_pair(y3, c3)
    up.wait_recv()
    for z in range(2):
        csum[y1, z] += r1[0, z]
    up2 = links.push(csum.at[y1], r2.at[0], me.yd(1))
    down.wait_recv()
    for z in range(2):
        csum[y3, z + 2] += r1[1, z]
    down2 = links.push(csum.at[y3], r2.at[1], me.yd(3))
    add_pair(y, c0)
    gg.step2()

    def gp_multiply(i):
        g_hi, g_lo = split(gbuf[pl.ds(2 * i, 2)].reshape(256, 2304))
        gpp[:, i] = dot3(g_hi, g_lo, p_hi[...], p_lo[...]).reshape(4, 64, 576)

    gg.step3()
    gg.finish()
    pl.loop(0, 2)(gp_multiply)
    gpc = [links.push(gpp.at[(x + d) % 4], gpx.at[d - 1], me.xd(d)) for d in (1, 2, 3)]
    up2.wait_recv()
    down2.wait_recv()

    @pl.loop(0, 4)
    def _(z):
        csum[y, z] = csum[y, z] + (r2[0, z] + r2[1, z])

    zc = [links.push(csum.at[y, (zl + d) % 4], rz.at[d - 1], me.zd(d)) for d in (1, 2, 3)]

    for r in range(8):
        pltpu.make_async_copy(xs.at[r], xs.at[r], recv.at[base_r + r]).wait()
    lane72 = lax.broadcasted_iota(jnp.int32, (72, 128), 1)
    flip = (col % 8) >= 4
    for m in range(4):
        b0, b1 = xs[2 * m], xs[2 * m + 1]
        first = jnp.where(lane72 < 64, b0, pltpu.roll(b1, 64, 1))
        second = jnp.where(lane72 < 64, pltpu.roll(b0, 64, 1), b1)
        x72[:, 128 * m:128 * m + 128] = jnp.where(flip, second, first)
    for copy in zc:
        copy.wait_recv()
    ybuf[y, zl, k] = csum[y, zl] + rz[0] + (rz[1] + rz[2])
    for copy in gpc:
        copy.wait_recv()
    gps[...] = gpp[x] + gpx[0] + (gpx[1] + gpx[2])
    gcopy = links.push(gps.at[1 - zh], gpa, me.anti())

    yv = ybuf[y, zl, k]
    for i, (top, left) in enumerate(((0, 0), (128, 0), (128, 256), (0, 128))):
        g = dot_full(x72[:, 128 * i:128 * i + 128], yv[:, :128 * i + 128], TN)
        gram[top // 128, :, :, :, left:left + 128 * i + 128] = g.reshape(4, 4, 8, 128 * i + 128)
    copy = links.push(gram.at[1 - k], gram_in, me.sib())
    copy.wait_recv()
    for i in range(4):
        ga[i] = gram[k, i] + gram_in[i]
    cs = [links.push(ga.at[(y + d) % 4], gy_in.at[d - 1], me.yd(d)) for d in (1, 2, 3)]
    gcopy.wait_recv()
    gp64[...] = gps[zh] + gpa[...]
    gp_hi, gp_lo = split(gp64[...])
    gyp[...] = dot3(gp_hi, gp_lo, xc_hi[...], xc_lo[...]).reshape(2, 4, 8, 512)
    ycopy = links.push(gyp.at[1 - k], gyd, me.sib())
    for copy in cs:
        copy.wait_recv()
    gb[...] = ga[y] + gy_in[0] + (gy_in[1] + gy_in[2])
    cs = [links.push(gb.at[(x + d) % 4], gx_in.at[d - 1], me.xd(d)) for d in (1, 2, 3)]
    ycopy.wait_recv()
    gya[...] = gyp[k] + gyd[...]
    ys = [links.push(gya.at[(y + d) % 4], gyy.at[d - 1], me.yd(d)) for d in (1, 2, 3)]
    for copy in cs:
        copy.wait_recv()
    gc[0] = gb[x] + gx_in[0] + (gx_in[1] + gx_in[2])
    cs = [links.push(gc.at[0], gz_in.at[d - 1], me.zd(d)) for d in (1, 2, 3)]
    for copy in ys:
        copy.wait_recv()
    gyb[...] = gya[y] + gyy[0] + (gyy[1] + gyy[2])
    ys = [links.push(gyb, gyz.at[d - 1], me.zd(d)) for d in (1, 2, 3)]
    for copy in cs:
        copy.wait_recv()
    gc[1] = gc[0] + gz_in[0] + (gz_in[1] + gz_in[2])
    copy = links.push(gc.at[1], gz_in.at[3], me.anti())
    for c in ys:
        c.wait_recv()
    gyo[k, y] = gyb[...] + gyz[0] + (gyz[1] + gyz[2])
    ys = [links.push(gyo.at[k, y], gyo.at[k, y], me.yd(d)) for d in (1, 2, 3)]
    copy.wait_recv()
    gout[k, y, x] = gc[1] + gz_in[3]
    cs = [links.push(gout.at[k, y, x], gout.at[k, y, x], me.xd(d)) for d in (1, 2, 3)]
    yg = PlaneGather(links, ybuf)
    yg.start()
    for copy in cs:
        copy.wait_recv()
    cs = [links.push(gout.at[k, y], gout.at[k, y], me.yd(d)) for d in (1, 2, 3)]
    for copy in ys:
        copy.wait_recv()
    ycopy = links.push(gyo.at[k], gyo.at[k], me.sib())
    for copy in cs:
        copy.wait_recv()
    copy = links.push(gout.at[k], gout.at[k], me.sib())
    yc = LooseCopy(links, ybuf.at[y, zl, k], ycb.at[col % 8], me.strip_source(col % 8), links.slot(), links.slot())
    ycopy.wait_recv()
    copy.wait_recv()

    ri = lax.broadcasted_iota(jnp.int32, (128, 128), 0)
    ci = lax.broadcasted_iota(jnp.int32, (128, 128), 1)
    for i, (top, left) in enumerate(((0, 0), (1, 0), (1, 256), (0, 128))):
        for j in range(i + 1):
            b = gout[top, :, :, :, left + 128 * j:left + 128 * j + 128].reshape(128, 128)
            if i == j:
                amat[128 * i:128 * i + 128, 128 * i:128 * i + 128] = b + jnp.where(ri == ci, 1.0, 0.0)
            else:
                amat[128 * i:128 * i + 128, 128 * j:128 * j + 128] = b
                amat[128 * j:128 * j + 128, 128 * i:128 * i + 128] = b.T

    def eliminate(j):
        at = pl.ds(pl.multiple_of(j * 128, 128), 128)
        inv = invert(amat[at, at])
        c = amat[:, at]
        r = dot_full(inv, amat[at, :])
        amat[...] -= dot_full(c, r)
        amat[:, at] = -dot_full(c, inv)
        amat[at, :] = r
        amat[at, at] = inv

    pl.loop(0, 1)(eliminate)
    yg.step1()
    yc.remote.wait_recv()
    ycg = RowGather(links, ycb)
    ycg.start()
    pl.loop(1, 2)(eliminate)
    yg.step2()
    ycg.step()
    pl.loop(2, 3)(eliminate)
    yg.step3()
    pl.loop(3, 4)(eliminate)
    yg.finish()
    out = pltpu.make_async_copy(ybuf, yr_hbm, lsem.at[1])
    out.start()
    ycg.finish()
    s_hi, s_lo = split(amat[...])

    @pl.loop(0, 2)
    def _(i):
        b_hi, b_lo = split(ycb[pl.ds(i * 4, 4)].reshape(288, 512))
        wt_ref[pl.ds(pl.multiple_of(i * 288, 288), 288), :] = dot3(b_hi, b_lo, s_hi, s_lo)

    gy_hi, gy_lo = split(gyo[...].reshape(64, 512))
    w_hi, w_lo = split(wt_ref[...])
    proj_ref[...] = gp64[...] - dot3(gy_hi, gy_lo, w_hi, w_lo, NT)
    out.wait()
    links.finish()


def mega_call(projector, saved, grad):
    vm = lambda *shape, dtype=F32: pltpu.VMEM(shape, dtype)
    scratch = [
        vm(576, 2304), vm(2304, 576, dtype=BF16), vm(2304, 576, dtype=BF16),
        vm(8, 288, 128), vm(8, 72, 128), vm(576, 512, dtype=BF16), vm(576, 512, dtype=BF16),
        vm(4, 4, 2, 16, 2304), vm(4, 4, 2, 72, 512), vm(4, 4, 72, 512), vm(4, 4, 72, 512),
        vm(2, 2, 72, 512), vm(2, 4, 72, 512), vm(3, 72, 512),
        vm(4, 4, 2, 72, 512), vm(8, 72, 512), vm(72, 512),
        vm(2, 4, 4, 8, 640), vm(4, 4, 8, 640), vm(4, 4, 8, 640), vm(3, 4, 8, 640),
        vm(4, 8, 640), vm(3, 8, 640), vm(2, 8, 640), vm(4, 8, 640), vm(2, 4, 4, 8, 640), vm(512, 512),
        vm(4, 2, 64, 576), vm(3, 2, 64, 576), vm(2, 64, 576), vm(64, 576), vm(64, 576),
        vm(2, 4, 8, 512), vm(4, 8, 512), vm(4, 8, 512), vm(3, 8, 512), vm(8, 512), vm(3, 8, 512), vm(2, 4, 8, 512),
        pltpu.SemaphoreType.DMA((NSEM,)), pltpu.SemaphoreType.DMA((NSEM,)), pltpu.SemaphoreType.DMA((2,)),
    ]
    anyspace = pl.BlockSpec(memory_space=pl.ANY)
    vmem = pl.BlockSpec(memory_space=pltpu.VMEM)
    return pl.pallas_call(
        mega,
        out_shape=[
            jax.ShapeDtypeStruct((4, 4, 2, 72, 512), F32),
            jax.ShapeDtypeStruct((576, 512), F32),
            jax.ShapeDtypeStruct((64, 576), F32),
        ],
        in_specs=[anyspace, vmem, vmem],
        out_specs=[anyspace, vmem, vmem],
        scratch_shapes=scratch,
        compiler_params=pltpu.CompilerParams(
            collective_id=0, has_side_effects=True, vmem_limit_bytes=58 * 1024 * 1024),
        name="solve",
    )(projector, saved, grad)


def update_kernel(p_ref, y_ref, wt_ref, o_ref, w_hi, w_lo):
    @pl.when(pl.program_id(0) == 0)
    def _():
        w_hi[...], w_lo[...] = split(wt_ref[...])

    y_hi, y_lo = split(y_ref[...])
    o_ref[...] = p_ref[...] - dot3(w_hi[...], w_lo[...], y_hi, y_lo, NT)


def update_call(projector, y_rows, wt):
    block = 256
    return pl.pallas_call(
        update_kernel,
        grid=(2304 // block,),
        out_shape=jax.ShapeDtypeStruct((576, 2304), F32),
        in_specs=[
            pl.BlockSpec((576, block), lambda i: (0, i)),
            pl.BlockSpec((block, 512), lambda i: (i, 0)),
            pl.BlockSpec((576, 512), lambda i: (0, 0)),
        ],
        out_specs=pl.BlockSpec((576, block), lambda i: (0, i)),
        scratch_shapes=[pltpu.VMEM((576, 512), BF16), pltpu.VMEM((576, 512), BF16)],
        compiler_params=pltpu.CompilerParams(vmem_limit_bytes=58 * 1024 * 1024),
        name="update",
    )(projector, y_rows, wt)


def local(projector, saved, grad_slab):
    turned = projector.T
    y_rows, wt, projected = mega_call(turned, saved.T, grad_slab)
    updated = update_call(turned, y_rows.reshape(2304, 512), wt)
    return (updated.T, projected)


def solution(mesh):
    return jax.shard_map(
        local,
        mesh=mesh,
        in_specs=(P("row", "col"), P("col", "row"), P("col", "row")),
        out_specs=(P("row", "col"), P("row", "col")),
        check_vma=False,
    )
```

```python
import functools

import jax
import jax.numpy as jnp
from jax import lax
from jax.experimental import pallas as pl
from jax.experimental.pallas import tpu as pltpu
from jax.sharding import PartitionSpec as P

MESH = pl.DeviceIdType.MESH
F32 = jnp.float32
BF16 = jnp.bfloat16
NN = (((1,), (0,)), ((), ()))
NT = (((1,), (1,)), ((), ()))
TN = (((0,), (0,)), ((), ()))


def split(x):
    hi = x.astype(BF16)
    return hi, (x - hi.astype(F32)).astype(BF16)


def dot3(a_hi, a_lo, b_hi, b_lo, dims=NN):
    dot = functools.partial(lax.dot_general, dimension_numbers=dims, preferred_element_type=F32)
    return dot(a_hi, b_hi) + (dot(a_hi, b_lo) + dot(a_lo, b_hi))


def dot_full(a, b, dims=NN):
    return lax.dot_general(a, b, dims, precision=lax.Precision.HIGHEST, preferred_element_type=F32)


class Place:
    def __init__(self):
        self.row = lax.axis_index("row")
        self.col = lax.axis_index("col")
        self.zh = self.row // 4
        self.x = self.row % 4
        self.y = self.col // 8
        self.zl = (self.col // 2) % 4
        self.k = self.col % 2

    def at(self, zh=None, x=None, y=None, zl=None, k=None):
        zh = self.zh if zh is None else zh
        x = self.x if x is None else x
        y = self.y if y is None else y
        zl = self.zl if zl is None else zl
        k = self.k if k is None else k
        return (zh * 4 + x, y * 8 + zl * 2 + k)

    def sib(self):
        return self.at(k=1 - self.k)

    def anti(self):
        return self.at(zh=1 - self.zh)

    def xd(self, d):
        return self.at(x=(self.x + d) % 4)

    def yd(self, d):
        return self.at(y=(self.y + d) % 4)

    def zd(self, d):
        return self.at(zl=(self.zl + d) % 4)

    def strip(self, q):
        return (self.col // 4, 8 * (self.col % 4) + q)

    def strip_source(self, r):
        return (r, 4 * self.row + self.col // 8)

    def is_me(self, dev):
        return jnp.logical_and(dev[0] == self.row, dev[1] == self.col)


class Links:
    def __init__(self, me, send, recv):
        self.me, self.send, self.recv, self.used = me, send, recv, 0
        self.sent = []

    def slot(self, n=1):
        self.used += n
        assert self.used <= NSEM, self.used
        return self.used - n

    def push(self, src, dst, dev):
        i = self.slot()
        copy = pltpu.make_async_remote_copy(
            src_ref=src, dst_ref=dst, send_sem=self.send.at[i], recv_sem=self.recv.at[i],
            device_id=dev, device_id_type=MESH)
        copy.start()
        self.sent.append(copy)
        return copy

    def finish(self):
        for copy in self.sent:
            copy.wait_send()


NSEM = 160


class PlaneGather:
    def __init__(self, links, buf):
        self.links, self.buf, self.me = links, buf, links.me

    def start(self):
        me, buf = self.me, self.buf
        mine = buf.at[me.y, me.zl, me.k]
        self.z = [self.links.push(mine, mine, me.zd(d)) for d in (1, 2, 3)]

    def pair(self, y):
        part = self.buf.at[y, :, self.me.k]
        copy = self.links.push(part, part, self.me.sib())
        self.pairs.append(copy)
        return copy

    def step1(self):
        me, buf = self.me, self.buf
        self.pairs = []
        for copy in self.z:
            copy.wait_recv()
        mine = buf.at[me.y, :, me.k]
        self.up = self.links.push(mine, mine, me.yd(1))
        self.down = self.links.push(mine, mine, me.yd(3))
        self.own = self.pair(me.y)

    def step2(self):
        me, buf = self.me, self.buf
        below, above = (me.y + 3) % 4, (me.y + 1) % 4
        self.up.wait_recv()
        half = buf.at[below, pl.ds(0, 2), me.k]
        self.up2 = self.links.push(half, half, me.yd(1))
        self.down.wait_recv()
        half = buf.at[above, pl.ds(2, 2), me.k]
        self.down2 = self.links.push(half, half, me.yd(3))
        self.below = self.pair(below)
        self.above = self.pair(above)

    def step3(self):
        self.up2.wait_recv()
        self.down2.wait_recv()
        self.last = self.pair((self.me.y + 2) % 4)

    def finish(self):
        for copy in self.pairs:
            copy.wait_recv()


class RowGather:
    def __init__(self, links, buf):
        self.links, self.buf, self.me = links, buf, links.me

    def start(self):
        me = self.me
        mine = self.buf.at[me.row]
        self.far = self.links.push(mine, mine, me.anti())
        self.near = [self.links.push(mine, mine, me.xd(d)) for d in (1, 2, 3)]

    def step(self):
        me = self.me
        self.far.wait_recv()
        other = self.buf.at[(me.row + 4) % 8]
        self.near2 = [self.links.push(other, other, me.xd(d)) for d in (1, 2, 3)]

    def finish(self):
        for copy in self.near + self.near2:
            copy.wait_recv()


def barrier(me):
    sem = pltpu.get_barrier_semaphore()
    devs = [me.sib(), me.anti()]
    devs += [f(d) for f in (me.xd, me.yd, me.zd) for d in (1, 2, 3)]
    for dev in devs:
        pl.semaphore_signal(sem, inc=1, device_id=dev, device_id_type=MESH)
    for dev in [me.strip_source(r) for r in range(8)] + [me.strip(me.row)]:

        @pl.when(jnp.logical_not(me.is_me(dev)))
        def _():
            pl.semaphore_signal(sem, inc=1, device_id=dev, device_id_type=MESH)

    count = jnp.int32(len(devs))
    for dev in [me.strip(q) for q in range(8)] + [me.strip_source(me.col % 8)]:
        count += jnp.where(me.is_me(dev), 0, 1)
    pl.semaphore_wait(sem, count)


class LooseCopy:
    def __init__(self, links, src, dst, dev, send, recv):
        me = links.me
        self.remote = pltpu.make_async_remote_copy(
            src_ref=src, dst_ref=dst, send_sem=links.send.at[send], recv_sem=links.recv.at[recv],
            device_id=dev, device_id_type=MESH)
        self.here = me.is_me(dev)
        self.local = pltpu.make_async_copy(src, dst, links.recv.at[recv])
        pl.when(jnp.logical_not(self.here))(lambda: self.remote.start())
        pl.when(self.here)(lambda: self.local.start())
        links.sent.append(self)

    def wait_send(self):
        pl.when(jnp.logical_not(self.here))(lambda: self.remote.wait_send())


def lanes(v, j):
    return jnp.broadcast_to(v[:, j:j + 1], (8, 128))


def rows8(v, i):
    return jnp.broadcast_to(v[i:i + 1, :], (8, 128))


def total(terms):
    while len(terms) > 1:
        terms = [a + b for a, b in zip(terms[::2], terms[1::2])]
    return terms[0]


def invert(a):
    s = lax.broadcasted_iota(jnp.int32, (8, 128), 0)
    lane = lax.broadcasted_iota(jnp.int32, (8, 128), 1)
    tiles = [a[8 * i:8 * i + 8, :] for i in range(16)]
    for g in range(16):
        e = [lanes(tiles[g], 8 * g + j) for j in range(8)]
        for i in range(8):
            p = 1.0 / rows8(e[i], i)
            new = []
            for j in range(8):
                if j == i:
                    new.append(jnp.where(s == i, p, -(e[i] * p)))
                else:
                    r = rows8(e[j], i) * p
                    new.append(jnp.where(s == i, r, e[j] - e[i] * r))
            e = new
        inside = jnp.logical_and(lane >= 8 * g, lane < 8 * g + 8)
        unit = jnp.where(inside, jnp.where(lane - 8 * g == s, 1.0, 0.0), tiles[g])
        pivot = total([e[j] * rows8(unit, j) for j in range(8)])
        each = [rows8(pivot, j) for j in range(8)]
        tiles = [
            pivot if i == g else jnp.where(inside, 0.0, t) - total([lanes(t, 8 * g + j) * each[j] for j in range(8)])
            for i, t in enumerate(tiles)
        ]
    return jnp.concatenate(tiles, axis=0)


def mega(p_hbm, xt_ref, g_ref, yr_hbm, wt_ref, proj_ref,
         pst, p_hi, p_lo, xbuf, xs, xc_hi, xc_lo, gbuf, part, d2d, csum, r1, r2, rz, ybuf, ycb, x72,
         gram, gram_in, ga, gy_in, gb, gx_in, gc, gz_in, gout, amat, gpp, gpx, gps, gpa, gp64,
         gyp, gyd, gya, gyy, gyb, gyz, gyo, send, recv, lsem):
    me = Place()
    row, col, zh, x, y, zl, k = me.row, me.col, me.zh, me.x, me.y, me.zl, me.k
    links = Links(me, send, recv)
    pcopy = pltpu.make_async_copy(p_hbm, pst, lsem.at[0])
    pcopy.start()
    xp_ref = xbuf.at[row]
    xp_ref[...] = jnp.concatenate([xt_ref[:, 0:288], xt_ref[:, 288:576]], axis=0).T
    gbuf[y, zl, k] = g_ref[...]
    barrier(me)
    xg = RowGather(links, xbuf)
    xg.start()
    gg = PlaneGather(links, gbuf)
    pcopy.wait()

    @pl.loop(0, 18)
    def _(i):
        rows = pl.ds(pl.multiple_of(i * 128, 128), 128)
        p_hi[rows], p_lo[rows] = split(pst[:, rows].T)

    xg.step()
    gg.start()
    lane = lax.broadcasted_iota(jnp.int32, (288, 128), 1)
    xg.finish()
    base_s, base_r = links.slot(8), links.slot(8)
    for q in range(8):
        LooseCopy(links, xp_ref.at[pl.ds(72 * (q % 4), 72)], xs.at[row], me.strip(q), base_s + q, base_r + row)
    for m in range(4):
        b0, b1 = xbuf[2 * m], xbuf[2 * m + 1]
        cols = pl.ds(128 * m, 128)
        xc_hi[0:288, cols], xc_lo[0:288, cols] = split(jnp.where(lane < 64, b0, pltpu.roll(b1, 64, 1)))
        xc_hi[288:576, cols], xc_lo[288:576, cols] = split(jnp.where(lane < 64, pltpu.roll(b0, 64, 1), b1))

    def multiply(ay):
        @pl.loop(0, 2)
        def _(z):
            rows = pl.ds(pl.multiple_of(ay * 576 + z * 288, 288), 288)
            part[ay, pl.ds(z * 2, 2)] = dot3(p_hi[rows], p_lo[rows], xc_hi[...], xc_lo[...]).reshape(2, 2, 72, 512)

        return links.push(part.at[ay, :, 1 - k], d2d.at[ay], me.sib())

    def add_pair(ay, copy):
        copy.wait_recv()

        @pl.loop(0, 4)
        def _(z):
            csum[ay, z] = part[ay, z, k] + d2d[ay, z]

    y1, y2, y3 = (y + 1) % 4, (y + 2) % 4, (y + 3) % 4
    c2 = multiply(y2)
    c1 = multiply(y1)
    add_pair(y2, c2)
    up = links.push(csum.at[y2, pl.ds(0, 2)], r1.at[0], me.yd(1))
    down = links.push(csum.at[y2, pl.ds(2, 2)], r1.at[1], me.yd(3))
    c3 = multiply(y3)
    add_pair(y1, c1)
    c0 = multiply(y)
    add_pair(y3, c3)
    up.wait_recv()
    for z in range(2):
        csum[y1, z] += r1[0, z]
    up2 = links.push(csum.at[y1], r2.at[0], me.yd(1))
    down.wait_recv()
    for z in range(2):
        csum[y3, z + 2] += r1[1, z]
    down2 = links.push(csum.at[y3], r2.at[1], me.yd(3))
    add_pair(y, c0)

    def gp_multiply(ay, copy):
        copy.wait_recv()
        g_hi, g_lo = split(gbuf[ay].reshape(128, 2304))
        gpp[pl.ds(2 * (ay % 2), 2), ay // 2] = dot3(g_hi, g_lo, p_hi[...], p_lo[...]).reshape(2, 64, 576)

    up2.wait_recv()
    down2.wait_recv()

    @pl.loop(0, 4)
    def _(z):
        csum[y, z] = csum[y, z] + (r2[0, z] + r2[1, z])

    zc = [links.push(csum.at[y, (zl + d) % 4], rz.at[d - 1], me.zd(d)) for d in (1, 2, 3)]
    gg.step1()

    for r in range(8):
        pltpu.make_async_copy(xs.at[r], xs.at[r], recv.at[base_r + r]).wait()
    lane72 = lax.broadcasted_iota(jnp.int32, (72, 128), 1)
    flip = (col % 8) >= 4
    for m in range(4):
        b0, b1 = xs[2 * m], xs[2 * m + 1]
        first = jnp.where(lane72 < 64, b0, pltpu.roll(b1, 64, 1))
        second = jnp.where(lane72 < 64, pltpu.roll(b0, 64, 1), b1)
        x72[:, 128 * m:128 * m + 128] = jnp.where(flip, second, first)
    gp_multiply(y, gg.own)
    for copy in zc:
        copy.wait_recv()
    ybuf[y, zl, k] = csum[y, zl] + rz[0] + (rz[1] + rz[2])

    yv = ybuf[y, zl, k]
    for i, (top, left) in enumerate(((0, 0), (128, 0), (128, 256), (0, 128))):
        g = dot_full(x72[:, 128 * i:128 * i + 128], yv[:, :128 * i + 128], TN)
        gram[top // 128, :, :, :, left:left + 128 * i + 128] = g.reshape(4, 4, 8, 128 * i + 128)
    copy = links.push(gram.at[1 - k], gram_in, me.sib())
    copy.wait_recv()
    for i in range(4):
        ga[i] = gram[k, i] + gram_in[i]
    cs = [links.push(ga.at[(y + d) % 4], gy_in.at[d - 1], me.yd(d)) for d in (1, 2, 3)]
    for copy in cs:
        copy.wait_recv()
    gb[...] = ga[y] + gy_in[0] + (gy_in[1] + gy_in[2])
    cs = [links.push(gb.at[(x + d) % 4], gx_in.at[d - 1], me.xd(d)) for d in (1, 2, 3)]
    gg.step2()
    for copy in cs:
        copy.wait_recv()
    gc[0] = gb[x] + gx_in[0] + (gx_in[1] + gx_in[2])
    cs = [links.push(gc.at[0], gz_in.at[d - 1], me.zd(d)) for d in (1, 2, 3)]
    gp_multiply((y + 1) % 4, gg.above)
    for copy in cs:
        copy.wait_recv()
    gc[1] = gc[0] + gz_in[0] + (gz_in[1] + gz_in[2])
    copy = links.push(gc.at[1], gz_in.at[3], me.anti())
    gg.step3()
    copy.wait_recv()
    gout[k, y, x] = gc[1] + gz_in[3]
    cs = [links.push(gout.at[k, y, x], gout.at[k, y, x], me.xd(d)) for d in (1, 2, 3)]
    yg = PlaneGather(links, ybuf)
    yg.start()
    gp_multiply((y + 3) % 4, gg.below)
    for copy in cs:
        copy.wait_recv()
    cs = [links.push(gout.at[k, y], gout.at[k, y], me.yd(d)) for d in (1, 2, 3)]
    gp_multiply((y + 2) % 4, gg.last)
    for copy in cs:
        copy.wait_recv()
    copy = links.push(gout.at[k], gout.at[k], me.sib())
    yc = LooseCopy(links, ybuf.at[y, zl, k], ycb.at[col % 8], me.strip_source(col % 8), links.slot(), links.slot())
    gpc = [links.push(gpp.at[(x + d) % 4], gpx.at[d - 1], me.xd(d)) for d in (1, 2, 3)]
    yg.step1()
    copy.wait_recv()

    ri = lax.broadcasted_iota(jnp.int32, (128, 128), 0)
    ci = lax.broadcasted_iota(jnp.int32, (128, 128), 1)
    for i, (top, left) in enumerate(((0, 0), (1, 0), (1, 256), (0, 128))):
        for j in range(i + 1):
            b = gout[top, :, :, :, left + 128 * j:left + 128 * j + 128].reshape(128, 128)
            if i == j:
                amat[128 * i:128 * i + 128, 128 * i:128 * i + 128] = b + jnp.where(ri == ci, 1.0, 0.0)
            else:
                amat[128 * i:128 * i + 128, 128 * j:128 * j + 128] = b
                amat[128 * j:128 * j + 128, 128 * i:128 * i + 128] = b.T

    def eliminate(j):
        at = pl.ds(pl.multiple_of(j * 128, 128), 128)
        inv = invert(amat[at, at])
        c = amat[:, at]
        r = dot_full(inv, amat[at, :])
        amat[...] -= dot_full(c, r)
        amat[:, at] = -dot_full(c, inv)
        amat[at, :] = r
        amat[at, at] = inv

    pl.loop(0, 1)(eliminate)
    yc.remote.wait_recv()
    ycg = RowGather(links, ycb)
    ycg.start()
    yg.step2()
    for copy in gpc:
        copy.wait_recv()
    gps[...] = gpp[x] + gpx[0] + (gpx[1] + gpx[2])
    gcopy = links.push(gps.at[1 - zh], gpa, me.anti())
    pl.loop(1, 2)(eliminate)
    ycg.step()
    yg.step3()
    gcopy.wait_recv()
    gp64[...] = gps[zh] + gpa[...]
    gp_hi, gp_lo = split(gp64[...])
    gyp[...] = dot3(gp_hi, gp_lo, xc_hi[...], xc_lo[...]).reshape(2, 4, 8, 512)
    copy = links.push(gyp.at[1 - k], gyd, me.sib())
    copy.wait_recv()
    gya[...] = gyp[k] + gyd[...]
    cs = [links.push(gya.at[(y + d) % 4], gyy.at[d - 1], me.yd(d)) for d in (1, 2, 3)]
    pl.loop(2, 3)(eliminate)
    for copy in cs:
        copy.wait_recv()
    gyb[...] = gya[y] + gyy[0] + (gyy[1] + gyy[2])
    cs = [links.push(gyb, gyz.at[d - 1], me.zd(d)) for d in (1, 2, 3)]
    yg.finish()
    out = pltpu.make_async_copy(ybuf, yr_hbm, lsem.at[1])
    out.start()
    for copy in cs:
        copy.wait_recv()
    gyo[k, y] = gyb[...] + gyz[0] + (gyz[1] + gyz[2])
    cs = [links.push(gyo.at[k, y], gyo.at[k, y], me.yd(d)) for d in (1, 2, 3)]
    pl.loop(3, 4)(eliminate)
    for copy in cs:
        copy.wait_recv()
    ycopy = links.push(gyo.at[k], gyo.at[k], me.sib())
    ycg.finish()
    s_hi, s_lo = split(amat[...])

    @pl.loop(0, 2)
    def _(i):
        b_hi, b_lo = split(ycb[pl.ds(i * 4, 4)].reshape(288, 512))
        wt_ref[pl.ds(pl.multiple_of(i * 288, 288), 288), :] = dot3(b_hi, b_lo, s_hi, s_lo)

    ycopy.wait_recv()
    gy_hi, gy_lo = split(gyo[...].reshape(64, 512))
    w_hi, w_lo = split(wt_ref[...])
    proj_ref[...] = gp64[...] - dot3(gy_hi, gy_lo, w_hi, w_lo, NT)
    out.wait()
    links.finish()


def mega_call(projector, saved, grad):
    vm = lambda *shape, dtype=F32: pltpu.VMEM(shape, dtype)
    scratch = [
        vm(576, 2304), vm(2304, 576, dtype=BF16), vm(2304, 576, dtype=BF16),
        vm(8, 288, 128), vm(8, 72, 128), vm(576, 512, dtype=BF16), vm(576, 512, dtype=BF16),
        vm(4, 4, 2, 16, 2304), vm(4, 4, 2, 72, 512), vm(4, 4, 72, 512), vm(4, 4, 72, 512),
        vm(2, 2, 72, 512), vm(2, 4, 72, 512), vm(3, 72, 512),
        vm(4, 4, 2, 72, 512), vm(8, 72, 512), vm(72, 512),
        vm(2, 4, 4, 8, 640), vm(4, 4, 8, 640), vm(4, 4, 8, 640), vm(3, 4, 8, 640),
        vm(4, 8, 640), vm(3, 8, 640), vm(2, 8, 640), vm(4, 8, 640), vm(2, 4, 4, 8, 640), vm(512, 512),
        vm(4, 2, 64, 576), vm(3, 2, 64, 576), vm(2, 64, 576), vm(64, 576), vm(64, 576),
        vm(2, 4, 8, 512), vm(4, 8, 512), vm(4, 8, 512), vm(3, 8, 512), vm(8, 512), vm(3, 8, 512), vm(2, 4, 8, 512),
        pltpu.SemaphoreType.DMA((NSEM,)), pltpu.SemaphoreType.DMA((NSEM,)), pltpu.SemaphoreType.DMA((2,)),
    ]
    anyspace = pl.BlockSpec(memory_space=pl.ANY)
    vmem = pl.BlockSpec(memory_space=pltpu.VMEM)
    return pl.pallas_call(
        mega,
        out_shape=[
            jax.ShapeDtypeStruct((4, 4, 2, 72, 512), F32),
            jax.ShapeDtypeStruct((576, 512), F32),
            jax.ShapeDtypeStruct((64, 576), F32),
        ],
        in_specs=[anyspace, vmem, vmem],
        out_specs=[anyspace, vmem, vmem],
        scratch_shapes=scratch,
        compiler_params=pltpu.CompilerParams(
            collective_id=0, has_side_effects=True, vmem_limit_bytes=58 * 1024 * 1024),
        name="solve",
    )(projector, saved, grad)


def update_kernel(p_ref, y_ref, wt_ref, o_ref, w):
    @pl.when(pl.program_id(0) == 0)
    def _():
        w_hi, w_lo = split(wt_ref[...])
        w[...] = jnp.concatenate([w_hi, w_hi, w_lo], axis=1)

    y_hi, y_lo = split(y_ref[...])
    y = jnp.concatenate([y_hi, y_lo, y_hi], axis=1)
    o_ref[...] = p_ref[...] - lax.dot_general(w[...], y, NT, preferred_element_type=F32)


def update_call(projector, y_rows, wt):
    block = 768
    return pl.pallas_call(
        update_kernel,
        grid=(2304 // block,),
        out_shape=jax.ShapeDtypeStruct((576, 2304), F32),
        in_specs=[
            pl.BlockSpec((576, block), lambda i: (0, i)),
            pl.BlockSpec((block, 512), lambda i: (i, 0)),
            pl.BlockSpec((576, 512), lambda i: (0, 0)),
        ],
        out_specs=pl.BlockSpec((576, block), lambda i: (0, i)),
        scratch_shapes=[pltpu.VMEM((576, 1536), BF16)],
        compiler_params=pltpu.CompilerParams(vmem_limit_bytes=58 * 1024 * 1024),
        name="update",
    )(projector, y_rows, wt)


def local(projector, saved, grad_slab):
    turned = projector.T
    y_rows, wt, projected = mega_call(turned, saved.T, grad_slab)
    updated = update_call(turned, y_rows.reshape(2304, 512), wt)
    return (updated.T, projected)


def solution(mesh):
    return jax.shard_map(
        local,
        mesh=mesh,
        in_specs=(P("row", "col"), P("col", "row"), P("col", "row")),
        out_specs=(P("row", "col"), P("row", "col")),
        check_vma=False,
    )
```

```python
import functools

import jax
import jax.numpy as jnp
from jax import lax
from jax.experimental import pallas as pl
from jax.experimental.pallas import tpu as pltpu
from jax.sharding import PartitionSpec as P

MESH = pl.DeviceIdType.MESH
F32 = jnp.float32
BF16 = jnp.bfloat16
NN = (((1,), (0,)), ((), ()))
NT = (((1,), (1,)), ((), ()))
TN = (((0,), (0,)), ((), ()))


def split(x):
    hi = x.astype(BF16)
    return hi, (x - hi.astype(F32)).astype(BF16)


def dot3(a_hi, a_lo, b_hi, b_lo, dims=NN):
    dot = functools.partial(lax.dot_general, dimension_numbers=dims, preferred_element_type=F32)
    return dot(a_hi, b_hi) + (dot(a_hi, b_lo) + dot(a_lo, b_hi))


def dot_full(a, b, dims=NN):
    return lax.dot_general(a, b, dims, precision=lax.Precision.HIGHEST, preferred_element_type=F32)


class Place:
    def __init__(self):
        self.row = lax.axis_index("row")
        self.col = lax.axis_index("col")
        self.zh = self.row // 4
        self.x = self.row % 4
        self.y = self.col // 8
        self.zl = (self.col // 2) % 4
        self.k = self.col % 2

    def at(self, zh=None, x=None, y=None, zl=None, k=None):
        zh = self.zh if zh is None else zh
        x = self.x if x is None else x
        y = self.y if y is None else y
        zl = self.zl if zl is None else zl
        k = self.k if k is None else k
        return (zh * 4 + x, y * 8 + zl * 2 + k)

    def sib(self):
        return self.at(k=1 - self.k)

    def anti(self):
        return self.at(zh=1 - self.zh)

    def xd(self, d):
        return self.at(x=(self.x + d) % 4)

    def yd(self, d):
        return self.at(y=(self.y + d) % 4)

    def zd(self, d):
        return self.at(zl=(self.zl + d) % 4)

    def strip(self, q):
        return (self.col // 4, 8 * (self.col % 4) + q)

    def strip_source(self, r):
        return (r, 4 * self.row + self.col // 8)

    def is_me(self, dev):
        return jnp.logical_and(dev[0] == self.row, dev[1] == self.col)


class Links:
    def __init__(self, me, send, recv):
        self.me, self.send, self.recv, self.used = me, send, recv, 0
        self.sent = []

    def slot(self, n=1):
        self.used += n
        assert self.used <= NSEM, self.used
        return self.used - n

    def push(self, src, dst, dev):
        i = self.slot()
        copy = pltpu.make_async_remote_copy(
            src_ref=src, dst_ref=dst, send_sem=self.send.at[i], recv_sem=self.recv.at[i],
            device_id=dev, device_id_type=MESH)
        copy.start()
        self.sent.append(copy)
        return copy

    def finish(self):
        for copy in self.sent:
            copy.wait_send()


NSEM = 200


class PlaneGather:
    def __init__(self, links, buf):
        self.links, self.buf, self.me = links, buf, links.me

    def start(self):
        me, buf = self.me, self.buf
        mine = buf.at[me.y, me.zl, me.k]
        self.z = [self.links.push(mine, mine, me.zd(d)) for d in (1, 2, 3)]

    def pair(self, y):
        part = self.buf.at[y, :, self.me.k]
        copy = self.links.push(part, part, self.me.sib())
        self.pairs.append(copy)
        return copy

    def step1(self):
        me, buf = self.me, self.buf
        self.pairs = []
        for copy in self.z:
            copy.wait_recv()
        mine = buf.at[me.y, :, me.k]
        self.up = self.links.push(mine, mine, me.yd(1))
        self.down = self.links.push(mine, mine, me.yd(3))
        self.own = self.pair(me.y)

    def step2(self):
        me, buf = self.me, self.buf
        below, above = (me.y + 3) % 4, (me.y + 1) % 4
        self.up.wait_recv()
        half = buf.at[below, pl.ds(0, 2), me.k]
        self.up2 = self.links.push(half, half, me.yd(1))
        self.down.wait_recv()
        half = buf.at[above, pl.ds(2, 2), me.k]
        self.down2 = self.links.push(half, half, me.yd(3))
        self.below = self.pair(below)
        self.above = self.pair(above)

    def step3(self):
        self.up2.wait_recv()
        self.down2.wait_recv()
        self.last = self.pair((self.me.y + 2) % 4)

    def finish(self):
        for copy in self.pairs:
            copy.wait_recv()


class RowGather:
    def __init__(self, links, buf):
        self.links, self.buf, self.me = links, buf, links.me

    def start(self):
        me = self.me
        mine = self.buf.at[me.row]
        self.far = self.links.push(mine, mine, me.anti())
        self.near = [self.links.push(mine, mine, me.xd(d)) for d in (1, 2, 3)]

    def step(self):
        me = self.me
        self.far.wait_recv()
        other = self.buf.at[(me.row + 4) % 8]
        self.near2 = [self.links.push(other, other, me.xd(d)) for d in (1, 2, 3)]

    def finish_near(self):
        for copy in self.near:
            copy.wait_recv()

    def finish_far(self):
        for copy in self.near2:
            copy.wait_recv()

    def finish(self):
        self.finish_near()
        self.finish_far()


def barrier(me):
    sem = pltpu.get_barrier_semaphore()
    devs = [me.sib(), me.anti()]
    devs += [f(d) for f in (me.xd, me.yd, me.zd) for d in (1, 2, 3)]
    for dev in devs:
        pl.semaphore_signal(sem, inc=1, device_id=dev, device_id_type=MESH)
    for dev in [me.strip_source(r) for r in range(8)] + [me.strip(me.row)]:

        @pl.when(jnp.logical_not(me.is_me(dev)))
        def _():
            pl.semaphore_signal(sem, inc=1, device_id=dev, device_id_type=MESH)

    count = jnp.int32(len(devs))
    for dev in [me.strip(q) for q in range(8)] + [me.strip_source(me.col % 8)]:
        count += jnp.where(me.is_me(dev), 0, 1)
    pl.semaphore_wait(sem, count)


class LooseCopy:
    def __init__(self, links, src, dst, dev, send, recv):
        me = links.me
        self.remote = pltpu.make_async_remote_copy(
            src_ref=src, dst_ref=dst, send_sem=links.send.at[send], recv_sem=links.recv.at[recv],
            device_id=dev, device_id_type=MESH)
        self.here = me.is_me(dev)
        self.local = pltpu.make_async_copy(src, dst, links.recv.at[recv])
        pl.when(jnp.logical_not(self.here))(lambda: self.remote.start())
        pl.when(self.here)(lambda: self.local.start())
        links.sent.append(self)

    def wait_send(self):
        pl.when(jnp.logical_not(self.here))(lambda: self.remote.wait_send())


def lanes(v, j):
    return jnp.broadcast_to(v[:, j:j + 1], (8, 128))


def rows8(v, i):
    return jnp.broadcast_to(v[i:i + 1, :], (8, 128))


def total(terms):
    while len(terms) > 1:
        terms = [a + b for a, b in zip(terms[::2], terms[1::2])]
    return terms[0]


def invert(a):
    s = lax.broadcasted_iota(jnp.int32, (8, 128), 0)
    lane = lax.broadcasted_iota(jnp.int32, (8, 128), 1)
    tiles = [a[8 * i:8 * i + 8, :] for i in range(16)]
    for g in range(16):
        e = [lanes(tiles[g], 8 * g + j) for j in range(8)]
        for i in range(8):
            p = 1.0 / rows8(e[i], i)
            new = []
            for j in range(8):
                if j == i:
                    new.append(jnp.where(s == i, p, -(e[i] * p)))
                else:
                    r = rows8(e[j], i) * p
                    new.append(jnp.where(s == i, r, e[j] - e[i] * r))
            e = new
        inside = jnp.logical_and(lane >= 8 * g, lane < 8 * g + 8)
        unit = jnp.where(inside, jnp.where(lane - 8 * g == s, 1.0, 0.0), tiles[g])
        pivot = total([e[j] * rows8(unit, j) for j in range(8)])
        each = [rows8(pivot, j) for j in range(8)]
        tiles = [
            pivot if i == g else jnp.where(inside, 0.0, t) - total([lanes(t, 8 * g + j) * each[j] for j in range(8)])
            for i, t in enumerate(tiles)
        ]
    return jnp.concatenate(tiles, axis=0)


def mega(p_hbm, xt_ref, g_ref, yr_hbm, wt_ref, proj_ref,
         pst, p_hi, p_lo, xbuf, xs, xc_hi, xc_lo, gbuf, part, d2d, csum, r1, r2, rz, ybuf, ycb, x72,
         gram, gram_in, ga, gy_in, gb, gx_in, gc, gz_in, gout, amat, gpp, gpx, gps, gpa, gp64,
         gyp, gyd, gya, gyy, gyb, gyz, gyo, send, recv, lsem):
    me = Place()
    row, col, zh, x, y, zl, k = me.row, me.col, me.zh, me.x, me.y, me.zl, me.k
    links = Links(me, send, recv)
    pcopy = pltpu.make_async_copy(p_hbm, pst, lsem.at[0])
    pcopy.start()
    xp_ref = xbuf.at[row]
    xp_ref[...] = jnp.concatenate([xt_ref[:, 0:288], xt_ref[:, 288:576]], axis=0).T
    gbuf[y, zl, k] = g_ref[...]
    barrier(me)
    xg = RowGather(links, xbuf)
    xg.start()
    gg = PlaneGather(links, gbuf)
    pcopy.wait()

    @pl.loop(0, 18)
    def _(i):
        rows = pl.ds(pl.multiple_of(i * 128, 128), 128)
        p_hi[rows], p_lo[rows] = split(pst[:, rows].T)

    xg.step()
    gg.start()
    lane = lax.broadcasted_iota(jnp.int32, (288, 128), 1)

    def assemble(h):
        group = zh if h == 0 else 1 - zh
        for m in range(2):
            b0, b1 = xbuf[4 * group + 2 * m], xbuf[4 * group + 2 * m + 1]
            cols = pl.ds(128 * m, 128)
            xc_hi[h, 0:288, cols], xc_lo[h, 0:288, cols] = split(jnp.where(lane < 64, b0, pltpu.roll(b1, 64, 1)))
            xc_hi[h, 288:576, cols], xc_lo[h, 288:576, cols] = split(jnp.where(lane < 64, pltpu.roll(b0, 64, 1), b1))

    y1, y2, y3 = (y + 1) % 4, (y + 2) % 4, (y + 3) % 4

    class Half:
        def __init__(self, h):
            self.h = h

        def multiply(self, ay):
            h = self.h

            @pl.loop(0, 2)
            def _(z):
                rows = pl.ds(pl.multiple_of(ay * 576 + z * 288, 288), 288)
                product = dot3(p_hi[rows], p_lo[rows], xc_hi[h], xc_lo[h])
                part[h, ay, pl.ds(z * 2, 2)] = product.reshape(2, 2, 72, 256)

            return links.push(part.at[h, ay, :, 1 - k], d2d.at[h, ay], me.sib())

        def add_pair(self, ay, copy):
            h = self.h
            copy.wait_recv()

            @pl.loop(0, 4)
            def _(z):
                csum[h, ay, z] = part[h, ay, z, k] + d2d[h, ay, z]

        def first(self):
            h = self.h
            c2 = self.multiply(y2)
            c1 = self.multiply(y1)
            self.add_pair(y2, c2)
            self.up = links.push(csum.at[h, y2, pl.ds(0, 2)], r1.at[h, 0], me.yd(1))
            self.down = links.push(csum.at[h, y2, pl.ds(2, 2)], r1.at[h, 1], me.yd(3))
            c3 = self.multiply(y3)
            self.add_pair(y1, c1)
            self.c0 = self.multiply(y)
            self.add_pair(y3, c3)

        def second(self):
            h = self.h
            self.up.wait_recv()
            for z in range(2):
                csum[h, y1, z] += r1[h, 0, z]
            self.up2 = links.push(csum.at[h, y1], r2.at[h, 0], me.yd(1))
            self.down.wait_recv()
            for z in range(2):
                csum[h, y3, z + 2] += r1[h, 1, z]
            self.down2 = links.push(csum.at[h, y3], r2.at[h, 1], me.yd(3))
            self.add_pair(y, self.c0)

        def third(self):
            h = self.h
            self.up2.wait_recv()
            self.down2.wait_recv()

            @pl.loop(0, 4)
            def _(z):
                csum[h, y, z] = csum[h, y, z] + (r2[h, 0, z] + r2[h, 1, z])

            self.zc = [links.push(csum.at[h, y, (zl + d) % 4], rz.at[h, d - 1], me.zd(d)) for d in (1, 2, 3)]

        def last(self):
            h = self.h
            for copy in self.zc:
                copy.wait_recv()
            group = zh if h == 0 else 1 - zh
            cols = pl.ds(pl.multiple_of(group * 256, 256), 256)
            ybuf[y, zl, k, :, cols] = csum[h, y, zl] + rz[h, 0] + (rz[h, 1] + rz[h, 2])

    near, far = Half(0), Half(1)
    xg.finish_near()
    assemble(0)
    near.first()
    xg.finish_far()
    base_s, base_r = links.slot(8), links.slot(8)
    for q in range(8):
        LooseCopy(links, xp_ref.at[pl.ds(72 * (q % 4), 72)], xs.at[row], me.strip(q), base_s + q, base_r + row)
    near.second()
    assemble(1)
    far.first()
    near.third()
    far.second()
    near.last()

    def gp_multiply(ay, copy):
        copy.wait_recv()
        g_hi, g_lo = split(gbuf[ay].reshape(128, 2304))
        gpp[pl.ds(2 * (ay % 2), 2), ay // 2] = dot3(g_hi, g_lo, p_hi[...], p_lo[...]).reshape(2, 64, 576)

    far.third()
    gg.step1()

    for r in range(8):
        pltpu.make_async_copy(xs.at[r], xs.at[r], recv.at[base_r + r]).wait()
    lane72 = lax.broadcasted_iota(jnp.int32, (72, 128), 1)
    flip = (col % 8) >= 4
    for m in range(4):
        b0, b1 = xs[2 * m], xs[2 * m + 1]
        first = jnp.where(lane72 < 64, b0, pltpu.roll(b1, 64, 1))
        second = jnp.where(lane72 < 64, pltpu.roll(b0, 64, 1), b1)
        x72[:, 128 * m:128 * m + 128] = jnp.where(flip, second, first)
    gp_multiply(y, gg.own)
    far.last()

    yv = ybuf[y, zl, k]
    for i, (top, left) in enumerate(((0, 0), (128, 0), (128, 256), (0, 128))):
        g = dot_full(x72[:, 128 * i:128 * i + 128], yv[:, :128 * i + 128], TN)
        gram[top // 128, :, :, :, left:left + 128 * i + 128] = g.reshape(4, 4, 8, 128 * i + 128)
    copy = links.push(gram.at[1 - k], gram_in, me.sib())
    copy.wait_recv()
    for i in range(4):
        ga[i] = gram[k, i] + gram_in[i]
    cs = [links.push(ga.at[(y + d) % 4], gy_in.at[d - 1], me.yd(d)) for d in (1, 2, 3)]
    for copy in cs:
        copy.wait_recv()
    gb[...] = ga[y] + gy_in[0] + (gy_in[1] + gy_in[2])
    cs = [links.push(gb.at[(x + d) % 4], gx_in.at[d - 1], me.xd(d)) for d in (1, 2, 3)]
    gg.step2()
    for copy in cs:
        copy.wait_recv()
    gc[0] = gb[x] + gx_in[0] + (gx_in[1] + gx_in[2])
    cs = [links.push(gc.at[0], gz_in.at[d - 1], me.zd(d)) for d in (1, 2, 3)]
    gp_multiply((y + 1) % 4, gg.above)
    for copy in cs:
        copy.wait_recv()
    gc[1] = gc[0] + gz_in[0] + (gz_in[1] + gz_in[2])
    copy = links.push(gc.at[1], gz_in.at[3], me.anti())
    gg.step3()
    copy.wait_recv()
    gout[k, y, x] = gc[1] + gz_in[3]
    cs = [links.push(gout.at[k, y, x], gout.at[k, y, x], me.xd(d)) for d in (1, 2, 3)]
    yg = PlaneGather(links, ybuf)
    yg.start()
    gp_multiply((y + 3) % 4, gg.below)
    for copy in cs:
        copy.wait_recv()
    cs = [links.push(gout.at[k, y], gout.at[k, y], me.yd(d)) for d in (1, 2, 3)]
    gp_multiply((y + 2) % 4, gg.last)
    for copy in cs:
        copy.wait_recv()
    copy = links.push(gout.at[k], gout.at[k], me.sib())
    yc = LooseCopy(links, ybuf.at[y, zl, k], ycb.at[col % 8], me.strip_source(col % 8), links.slot(), links.slot())
    gpc = [links.push(gpp.at[(x + d) % 4], gpx.at[d - 1], me.xd(d)) for d in (1, 2, 3)]
    yg.step1()
    copy.wait_recv()

    ri = lax.broadcasted_iota(jnp.int32, (128, 128), 0)
    ci = lax.broadcasted_iota(jnp.int32, (128, 128), 1)
    for i, (top, left) in enumerate(((0, 0), (1, 0), (1, 256), (0, 128))):
        for j in range(i + 1):
            b = gout[top, :, :, :, left + 128 * j:left + 128 * j + 128].reshape(128, 128)
            if i == j:
                amat[128 * i:128 * i + 128, 128 * i:128 * i + 128] = b + jnp.where(ri == ci, 1.0, 0.0)
            else:
                amat[128 * i:128 * i + 128, 128 * j:128 * j + 128] = b
                amat[128 * j:128 * j + 128, 128 * i:128 * i + 128] = b.T

    def eliminate(j):
        at = pl.ds(pl.multiple_of(j * 128, 128), 128)
        inv = invert(amat[at, at])
        c = amat[:, at]
        r = dot_full(inv, amat[at, :])
        amat[...] -= dot_full(c, r)
        amat[:, at] = -dot_full(c, inv)
        amat[at, :] = r
        amat[at, at] = inv

    pl.loop(0, 1)(eliminate)
    yc.remote.wait_recv()
    ycg = RowGather(links, ycb)
    ycg.start()
    yg.step2()
    for copy in gpc:
        copy.wait_recv()
    gps[...] = gpp[x] + gpx[0] + (gpx[1] + gpx[2])
    gcopy = links.push(gps.at[1 - zh], gpa, me.anti())
    pl.loop(1, 2)(eliminate)
    ycg.step()
    yg.step3()
    gcopy.wait_recv()
    gp64[...] = gps[zh] + gpa[...]
    gp_hi, gp_lo = split(gp64[...])
    for h in range(2):
        cols = pl.ds(pl.multiple_of((zh if h == 0 else 1 - zh) * 256, 256), 256)
        gyp[:, :, :, cols] = dot3(gp_hi, gp_lo, xc_hi[h], xc_lo[h]).reshape(2, 4, 8, 256)
    copy = links.push(gyp.at[1 - k], gyd, me.sib())
    copy.wait_recv()
    gya[...] = gyp[k] + gyd[...]
    cs = [links.push(gya.at[(y + d) % 4], gyy.at[d - 1], me.yd(d)) for d in (1, 2, 3)]
    pl.loop(2, 3)(eliminate)
    for copy in cs:
        copy.wait_recv()
    gyb[...] = gya[y] + gyy[0] + (gyy[1] + gyy[2])
    cs = [links.push(gyb, gyz.at[d - 1], me.zd(d)) for d in (1, 2, 3)]
    yg.finish()
    out = pltpu.make_async_copy(ybuf, yr_hbm, lsem.at[1])
    out.start()
    for copy in cs:
        copy.wait_recv()
    gyo[k, y] = gyb[...] + gyz[0] + (gyz[1] + gyz[2])
    cs = [links.push(gyo.at[k, y], gyo.at[k, y], me.yd(d)) for d in (1, 2, 3)]
    pl.loop(3, 4)(eliminate)
    for copy in cs:
        copy.wait_recv()
    ycopy = links.push(gyo.at[k], gyo.at[k], me.sib())
    ycg.finish()
    s_hi, s_lo = split(amat[...])

    @pl.loop(0, 2)
    def _(i):
        b_hi, b_lo = split(ycb[pl.ds(i * 4, 4)].reshape(288, 512))
        wt_ref[pl.ds(pl.multiple_of(i * 288, 288), 288), :] = dot3(b_hi, b_lo, s_hi, s_lo)

    ycopy.wait_recv()
    gy_hi, gy_lo = split(gyo[...].reshape(64, 512))
    w_hi, w_lo = split(wt_ref[...])
    proj_ref[...] = gp64[...] - dot3(gy_hi, gy_lo, w_hi, w_lo, NT)
    out.wait()
    links.finish()


def mega_call(projector, saved, grad):
    vm = lambda *shape, dtype=F32: pltpu.VMEM(shape, dtype)
    scratch = [
        vm(576, 2304), vm(2304, 576, dtype=BF16), vm(2304, 576, dtype=BF16),
        vm(8, 288, 128), vm(8, 72, 128), vm(2, 576, 256, dtype=BF16), vm(2, 576, 256, dtype=BF16),
        vm(4, 4, 2, 16, 2304), vm(2, 4, 4, 2, 72, 256), vm(2, 4, 4, 72, 256), vm(2, 4, 4, 72, 256),
        vm(2, 2, 2, 72, 256), vm(2, 2, 4, 72, 256), vm(2, 3, 72, 256),
        vm(4, 4, 2, 72, 512), vm(8, 72, 512), vm(72, 512),
        vm(2, 4, 4, 8, 640), vm(4, 4, 8, 640), vm(4, 4, 8, 640), vm(3, 4, 8, 640),
        vm(4, 8, 640), vm(3, 8, 640), vm(2, 8, 640), vm(4, 8, 640), vm(2, 4, 4, 8, 640), vm(512, 512),
        vm(4, 2, 64, 576), vm(3, 2, 64, 576), vm(2, 64, 576), vm(64, 576), vm(64, 576),
        vm(2, 4, 8, 512), vm(4, 8, 512), vm(4, 8, 512), vm(3, 8, 512), vm(8, 512), vm(3, 8, 512), vm(2, 4, 8, 512),
        pltpu.SemaphoreType.DMA((NSEM,)), pltpu.SemaphoreType.DMA((NSEM,)), pltpu.SemaphoreType.DMA((2,)),
    ]
    anyspace = pl.BlockSpec(memory_space=pl.ANY)
    vmem = pl.BlockSpec(memory_space=pltpu.VMEM)
    return pl.pallas_call(
        mega,
        out_shape=[
            jax.ShapeDtypeStruct((4, 4, 2, 72, 512), F32),
            jax.ShapeDtypeStruct((576, 512), F32),
            jax.ShapeDtypeStruct((64, 576), F32),
        ],
        in_specs=[anyspace, vmem, vmem],
        out_specs=[anyspace, vmem, vmem],
        scratch_shapes=scratch,
        compiler_params=pltpu.CompilerParams(
            collective_id=0, has_side_effects=True, vmem_limit_bytes=58 * 1024 * 1024),
        name="solve",
    )(projector, saved, grad)


def update_kernel(p_ref, y_ref, wt_ref, o_ref, w):
    @pl.when(pl.program_id(0) == 0)
    def _():
        w_hi, w_lo = split(wt_ref[...])
        w[...] = jnp.concatenate([w_hi, w_hi, w_lo], axis=1)

    y_hi, y_lo = split(y_ref[...])
    y = jnp.concatenate([y_hi, y_lo, y_hi], axis=1)
    o_ref[...] = p_ref[...] - lax.dot_general(w[...], y, NT, preferred_element_type=F32)


def update_call(projector, y_rows, wt):
    block = 768
    return pl.pallas_call(
        update_kernel,
        grid=(2304 // block,),
        out_shape=jax.ShapeDtypeStruct((576, 2304), F32),
        in_specs=[
            pl.BlockSpec((576, block), lambda i: (0, i)),
            pl.BlockSpec((block, 512), lambda i: (i, 0)),
            pl.BlockSpec((576, 512), lambda i: (0, 0)),
        ],
        out_specs=pl.BlockSpec((576, block), lambda i: (0, i)),
        scratch_shapes=[pltpu.VMEM((576, 1536), BF16)],
        compiler_params=pltpu.CompilerParams(vmem_limit_bytes=58 * 1024 * 1024),
        name="update",
    )(projector, y_rows, wt)


def local(projector, saved, grad_slab):
    turned = projector.T
    y_rows, wt, projected = mega_call(turned, saved.T, grad_slab)
    updated = update_call(turned, y_rows.reshape(2304, 512), wt)
    return (updated.T, projected)


def solution(mesh):
    return jax.shard_map(
        local,
        mesh=mesh,
        in_specs=(P("row", "col"), P("col", "row"), P("col", "row")),
        out_specs=(P("row", "col"), P("row", "col")),
        check_vma=False,
    )
```

```python
import functools

import jax
import jax.numpy as jnp
from jax import lax
from jax.experimental import pallas as pl
from jax.experimental.pallas import tpu as pltpu
from jax.sharding import PartitionSpec as P

MESH = pl.DeviceIdType.MESH
F32 = jnp.float32
BF16 = jnp.bfloat16
NN = (((1,), (0,)), ((), ()))
NT = (((1,), (1,)), ((), ()))
TN = (((0,), (0,)), ((), ()))


def split(x):
    hi = x.astype(BF16)
    return hi, (x - hi.astype(F32)).astype(BF16)


def dot3(a_hi, a_lo, b_hi, b_lo, dims=NN):
    dot = functools.partial(lax.dot_general, dimension_numbers=dims, preferred_element_type=F32)
    return dot(a_hi, b_hi) + (dot(a_hi, b_lo) + dot(a_lo, b_hi))


def dot_full(a, b, dims=NN):
    return lax.dot_general(a, b, dims, precision=lax.Precision.HIGHEST, preferred_element_type=F32)


class Place:
    def __init__(self):
        self.row = lax.axis_index("row")
        self.col = lax.axis_index("col")
        self.zh = self.row // 4
        self.x = self.row % 4
        self.y = self.col // 8
        self.zl = (self.col // 2) % 4
        self.k = self.col % 2

    def at(self, zh=None, x=None, y=None, zl=None, k=None):
        zh = self.zh if zh is None else zh
        x = self.x if x is None else x
        y = self.y if y is None else y
        zl = self.zl if zl is None else zl
        k = self.k if k is None else k
        return (zh * 4 + x, y * 8 + zl * 2 + k)

    def sib(self):
        return self.at(k=1 - self.k)

    def anti(self):
        return self.at(zh=1 - self.zh)

    def xd(self, d):
        return self.at(x=(self.x + d) % 4)

    def yd(self, d):
        return self.at(y=(self.y + d) % 4)

    def zd(self, d):
        return self.at(zl=(self.zl + d) % 4)

    def strip(self, q):
        return (self.col // 4, 8 * (self.col % 4) + q)

    def strip_source(self, r):
        return (r, 4 * self.row + self.col // 8)

    def is_me(self, dev):
        return jnp.logical_and(dev[0] == self.row, dev[1] == self.col)


class Links:
    def __init__(self, me, send, recv):
        self.me, self.send, self.recv, self.used = me, send, recv, 0
        self.sent = []

    def slot(self, n=1):
        self.used += n
        assert self.used <= NSEM, self.used
        return self.used - n

    def push(self, src, dst, dev):
        i = self.slot()
        copy = pltpu.make_async_remote_copy(
            src_ref=src, dst_ref=dst, send_sem=self.send.at[i], recv_sem=self.recv.at[i],
            device_id=dev, device_id_type=MESH)
        copy.start()
        self.sent.append(copy)
        return copy

    def finish(self):
        for copy in self.sent:
            copy.wait_send()


NSEM = 200


class PlaneGather:
    def __init__(self, links, buf):
        self.links, self.buf, self.me = links, buf, links.me

    def start(self):
        me, buf = self.me, self.buf
        mine = buf.at[me.y, me.zl, me.k]
        self.z = [self.links.push(mine, mine, me.zd(d)) for d in (1, 2, 3)]

    def pair(self, y):
        part = self.buf.at[y, :, self.me.k]
        copy = self.links.push(part, part, self.me.sib())
        self.pairs.append(copy)
        return copy

    def step1(self):
        me, buf = self.me, self.buf
        self.pairs = []
        for copy in self.z:
            copy.wait_recv()
        mine = buf.at[me.y, :, me.k]
        self.up = self.links.push(mine, mine, me.yd(1))
        self.down = self.links.push(mine, mine, me.yd(3))
        self.own = self.pair(me.y)

    def step2(self):
        me, buf = self.me, self.buf
        below, above = (me.y + 3) % 4, (me.y + 1) % 4
        self.up.wait_recv()
        half = buf.at[below, pl.ds(0, 2), me.k]
        self.up2 = self.links.push(half, half, me.yd(1))
        self.down.wait_recv()
        half = buf.at[above, pl.ds(2, 2), me.k]
        self.down2 = self.links.push(half, half, me.yd(3))
        self.below = self.pair(below)
        self.above = self.pair(above)

    def step3(self):
        self.up2.wait_recv()
        self.down2.wait_recv()
        self.last = self.pair((self.me.y + 2) % 4)

    def finish(self):
        for copy in self.pairs:
            copy.wait_recv()


class RowGather:
    def __init__(self, links, buf):
        self.links, self.buf, self.me = links, buf, links.me

    def start(self):
        me = self.me
        mine = self.buf.at[me.row]
        self.far = self.links.push(mine, mine, me.anti())
        self.near = [self.links.push(mine, mine, me.xd(d)) for d in (1, 2, 3)]

    def step(self):
        me = self.me
        self.far.wait_recv()
        other = self.buf.at[(me.row + 4) % 8]
        self.near2 = [self.links.push(other, other, me.xd(d)) for d in (1, 2, 3)]

    def finish_near(self):
        for copy in self.near:
            copy.wait_recv()

    def finish_far(self):
        for copy in self.near2:
            copy.wait_recv()

    def finish(self):
        self.finish_near()
        self.finish_far()


def barrier(me):
    sem = pltpu.get_barrier_semaphore()
    devs = [me.sib(), me.anti()]
    devs += [f(d) for f in (me.xd, me.yd, me.zd) for d in (1, 2, 3)]
    for dev in devs:
        pl.semaphore_signal(sem, inc=1, device_id=dev, device_id_type=MESH)
    for dev in [me.strip_source(r) for r in range(8)] + [me.strip(me.row)]:

        @pl.when(jnp.logical_not(me.is_me(dev)))
        def _():
            pl.semaphore_signal(sem, inc=1, device_id=dev, device_id_type=MESH)

    count = jnp.int32(len(devs))
    for dev in [me.strip(q) for q in range(8)] + [me.strip_source(me.col % 8)]:
        count += jnp.where(me.is_me(dev), 0, 1)
    pl.semaphore_wait(sem, count)


class LooseCopy:
    def __init__(self, links, src, dst, dev, send, recv):
        me = links.me
        self.remote = pltpu.make_async_remote_copy(
            src_ref=src, dst_ref=dst, send_sem=links.send.at[send], recv_sem=links.recv.at[recv],
            device_id=dev, device_id_type=MESH)
        self.here = me.is_me(dev)
        self.local = pltpu.make_async_copy(src, dst, links.recv.at[recv])
        pl.when(jnp.logical_not(self.here))(lambda: self.remote.start())
        pl.when(self.here)(lambda: self.local.start())
        links.sent.append(self)

    def wait_send(self):
        pl.when(jnp.logical_not(self.here))(lambda: self.remote.wait_send())


def lanes(v, j):
    return jnp.broadcast_to(v[:, j:j + 1], (8, 128))


def rows8(v, i):
    return jnp.broadcast_to(v[i:i + 1, :], (8, 128))


def total(terms):
    while len(terms) > 1:
        terms = [a + b for a, b in zip(terms[::2], terms[1::2])]
    return terms[0]


def invert(a):
    s = lax.broadcasted_iota(jnp.int32, (8, 128), 0)
    lane = lax.broadcasted_iota(jnp.int32, (8, 128), 1)
    tiles = [a[8 * i:8 * i + 8, :] for i in range(16)]
    for g in range(16):
        e = [lanes(tiles[g], 8 * g + j) for j in range(8)]
        for i in range(8):
            p = 1.0 / rows8(e[i], i)
            new = []
            for j in range(8):
                if j == i:
                    new.append(jnp.where(s == i, p, -(e[i] * p)))
                else:
                    r = rows8(e[j], i) * p
                    new.append(jnp.where(s == i, r, e[j] - e[i] * r))
            e = new
        inside = jnp.logical_and(lane >= 8 * g, lane < 8 * g + 8)
        unit = jnp.where(inside, jnp.where(lane - 8 * g == s, 1.0, 0.0), tiles[g])
        pivot = total([e[j] * rows8(unit, j) for j in range(8)])
        each = [rows8(pivot, j) for j in range(8)]
        tiles = [
            pivot if i == g else jnp.where(inside, 0.0, t) - total([lanes(t, 8 * g + j) * each[j] for j in range(8)])
            for i, t in enumerate(tiles)
        ]
    return jnp.concatenate(tiles, axis=0)


def mega(p_hbm, xt_ref, g_ref, yr_hbm, wt_ref, proj_ref,
         pst, p_hi, p_lo, xbuf, xs, xc_hi, xc_lo, gbuf, part, d2d, csum, r1, r2, rz, ybuf, ycb, x72,
         gram, gram_in, ga, gy_in, gb, gx_in, gc, gz_in, gout, amat, gpp, gpx, gps, gpa, gp64,
         gyp, gyd, gya, gyy, gyb, gyz, gyo, send, recv, lsem):
    me = Place()
    row, col, zh, x, y, zl, k = me.row, me.col, me.zh, me.x, me.y, me.zl, me.k
    links = Links(me, send, recv)
    pcopy = pltpu.make_async_copy(p_hbm, pst, lsem.at[0])
    pcopy.start()
    xp_ref = xbuf.at[row]
    xp_ref[...] = jnp.concatenate([xt_ref[:, 0:288], xt_ref[:, 288:576]], axis=0).T
    gbuf[y, zl, k] = g_ref[...]
    barrier(me)
    xg = RowGather(links, xbuf)
    xg.start()
    gg = PlaneGather(links, gbuf)
    pcopy.wait()

    @pl.loop(0, 18)
    def _(i):
        rows = pl.ds(pl.multiple_of(i * 128, 128), 128)
        p_hi[rows], p_lo[rows] = split(pst[:, rows].T)

    xg.step()
    gg.start()
    lane = lax.broadcasted_iota(jnp.int32, (288, 128), 1)

    def assemble(h):
        group = zh if h == 0 else 1 - zh
        for m in range(2):
            b0, b1 = xbuf[4 * group + 2 * m], xbuf[4 * group + 2 * m + 1]
            cols = pl.ds(128 * m, 128)
            xc_hi[h, 0:288, cols], xc_lo[h, 0:288, cols] = split(jnp.where(lane < 64, b0, pltpu.roll(b1, 64, 1)))
            xc_hi[h, 288:576, cols], xc_lo[h, 288:576, cols] = split(jnp.where(lane < 64, pltpu.roll(b0, 64, 1), b1))

    y1, y2, y3 = (y + 1) % 4, (y + 2) % 4, (y + 3) % 4

    class Half:
        def __init__(self, h):
            self.h = h

        def multiply(self, ay):
            h = self.h

            @pl.loop(0, 2)
            def _(z):
                rows = pl.ds(pl.multiple_of(ay * 576 + z * 288, 288), 288)
                product = dot3(p_hi[rows], p_lo[rows], xc_hi[h], xc_lo[h])
                part[h, ay, pl.ds(z * 2, 2)] = product.reshape(2, 2, 72, 256)

            return links.push(part.at[h, ay, :, 1 - k], d2d.at[h, ay], me.sib())

        def add_pair(self, ay, copy):
            h = self.h
            copy.wait_recv()

            @pl.loop(0, 4)
            def _(z):
                csum[h, ay, z] = part[h, ay, z, k] + d2d[h, ay, z]

        def first(self):
            h = self.h
            c2 = self.multiply(y2)
            c1 = self.multiply(y1)
            self.add_pair(y2, c2)
            self.up = links.push(csum.at[h, y2, pl.ds(0, 2)], r1.at[h, 0], me.yd(1))
            self.down = links.push(csum.at[h, y2, pl.ds(2, 2)], r1.at[h, 1], me.yd(3))
            c3 = self.multiply(y3)
            self.add_pair(y1, c1)
            self.c0 = self.multiply(y)
            self.add_pair(y3, c3)

        def second(self):
            h = self.h
            self.up.wait_recv()
            for z in range(2):
                csum[h, y1, z] += r1[h, 0, z]
            self.up2 = links.push(csum.at[h, y1], r2.at[h, 0], me.yd(1))
            self.down.wait_recv()
            for z in range(2):
                csum[h, y3, z + 2] += r1[h, 1, z]
            self.down2 = links.push(csum.at[h, y3], r2.at[h, 1], me.yd(3))
            self.add_pair(y, self.c0)

        def third(self):
            h = self.h
            self.up2.wait_recv()
            self.down2.wait_recv()

            @pl.loop(0, 4)
            def _(z):
                csum[h, y, z] = csum[h, y, z] + (r2[h, 0, z] + r2[h, 1, z])

            self.zc = [links.push(csum.at[h, y, (zl + d) % 4], rz.at[h, d - 1], me.zd(d)) for d in (1, 2, 3)]

        def last(self):
            h = self.h
            for copy in self.zc:
                copy.wait_recv()
            group = zh if h == 0 else 1 - zh
            cols = pl.ds(pl.multiple_of(group * 256, 256), 256)
            ybuf[y, zl, k, :, cols] = csum[h, y, zl] + rz[h, 0] + (rz[h, 1] + rz[h, 2])

    near, far = Half(0), Half(1)
    xg.finish_near()
    assemble(0)
    near.first()
    xg.finish_far()
    base_s, base_r = links.slot(8), links.slot(8)
    for q in range(8):
        LooseCopy(links, xp_ref.at[pl.ds(72 * (q % 4), 72)], xs.at[row], me.strip(q), base_s + q, base_r + row)
    near.second()
    assemble(1)
    far.first()
    near.third()
    far.second()
    near.last()

    def gp_multiply(ay, copy):
        copy.wait_recv()
        g_hi, g_lo = split(gbuf[ay].reshape(128, 2304))
        gpp[pl.ds(2 * (ay % 2), 2), ay // 2] = dot3(g_hi, g_lo, p_hi[...], p_lo[...]).reshape(2, 64, 576)

    far.third()
    gg.step1()

    for r in range(8):
        pltpu.make_async_copy(xs.at[r], xs.at[r], recv.at[base_r + r]).wait()
    lane72 = lax.broadcasted_iota(jnp.int32, (72, 128), 1)
    flip = (col % 8) >= 4
    for m in range(4):
        b0, b1 = xs[2 * m], xs[2 * m + 1]
        first = jnp.where(lane72 < 64, b0, pltpu.roll(b1, 64, 1))
        second = jnp.where(lane72 < 64, pltpu.roll(b0, 64, 1), b1)
        x72[:, 128 * m:128 * m + 128] = jnp.where(flip, second, first)
    gp_multiply(y, gg.own)
    far.last()
    yc = LooseCopy(links, ybuf.at[y, zl, k], ycb.at[col % 8], me.strip_source(col % 8), links.slot(), links.slot())

    yv = ybuf[y, zl, k]
    for i, (top, left) in enumerate(((0, 0), (128, 0), (128, 256), (0, 128))):
        g = dot_full(x72[:, 128 * i:128 * i + 128], yv[:, :128 * i + 128], TN)
        gram[top // 128, :, :, :, left:left + 128 * i + 128] = g.reshape(4, 4, 8, 128 * i + 128)
    copy = links.push(gram.at[1 - k], gram_in, me.sib())
    copy.wait_recv()
    for i in range(4):
        ga[i] = gram[k, i] + gram_in[i]
    cs = [links.push(ga.at[(y + d) % 4], gy_in.at[d - 1], me.yd(d)) for d in (1, 2, 3)]
    for copy in cs:
        copy.wait_recv()
    gb[...] = ga[y] + gy_in[0] + (gy_in[1] + gy_in[2])
    cs = [links.push(gb.at[(x + d) % 4], gx_in.at[d - 1], me.xd(d)) for d in (1, 2, 3)]
    gg.step2()
    for copy in cs:
        copy.wait_recv()
    gc[0] = gb[x] + gx_in[0] + (gx_in[1] + gx_in[2])
    cs = [links.push(gc.at[0], gz_in.at[d - 1], me.zd(d)) for d in (1, 2, 3)]
    gp_multiply((y + 1) % 4, gg.above)
    for copy in cs:
        copy.wait_recv()
    gc[1] = gc[0] + gz_in[0] + (gz_in[1] + gz_in[2])
    copy = links.push(gc.at[1], gz_in.at[3], me.anti())
    gg.step3()
    copy.wait_recv()
    gout[k, y, x] = gc[1] + gz_in[3]
    cs = [links.push(gout.at[k, y, x], gout.at[k, y, x], me.xd(d)) for d in (1, 2, 3)]
    yg = PlaneGather(links, ybuf)
    yg.start()
    gp_multiply((y + 3) % 4, gg.below)
    for copy in cs:
        copy.wait_recv()
    cs = [links.push(gout.at[k, y], gout.at[k, y], me.yd(d)) for d in (1, 2, 3)]
    gp_multiply((y + 2) % 4, gg.last)
    for copy in cs:
        copy.wait_recv()
    copy = links.push(gout.at[k], gout.at[k], me.sib())
    gpc = [links.push(gpp.at[(x + d) % 4], gpx.at[d - 1], me.xd(d)) for d in (1, 2, 3)]
    yc.remote.wait_recv()
    ycg = RowGather(links, ycb)
    ycg.start()
    yg.step1()
    copy.wait_recv()

    ri = lax.broadcasted_iota(jnp.int32, (128, 128), 0)
    ci = lax.broadcasted_iota(jnp.int32, (128, 128), 1)
    for i, (top, left) in enumerate(((0, 0), (1, 0), (1, 256), (0, 128))):
        for j in range(i + 1):
            b = gout[top, :, :, :, left + 128 * j:left + 128 * j + 128].reshape(128, 128)
            if i == j:
                amat[128 * i:128 * i + 128, 128 * i:128 * i + 128] = b + jnp.where(ri == ci, 1.0, 0.0)
            else:
                amat[128 * i:128 * i + 128, 128 * j:128 * j + 128] = b
                amat[128 * j:128 * j + 128, 128 * i:128 * i + 128] = b.T

    def eliminate(j):
        at = pl.ds(pl.multiple_of(j * 128, 128), 128)
        inv = invert(amat[at, at])
        c = amat[:, at]
        r = dot_full(inv, amat[at, :])
        amat[...] -= dot_full(c, r)
        amat[:, at] = -dot_full(c, inv)
        amat[at, :] = r
        amat[at, at] = inv

    pl.loop(0, 1)(eliminate)
    yg.step2()
    ycg.step()
    pl.loop(1, 2)(eliminate)
    yg.step3()
    for copy in gpc:
        copy.wait_recv()
    gps[...] = gpp[x] + gpx[0] + (gpx[1] + gpx[2])
    gcopy = links.push(gps.at[1 - zh], gpa, me.anti())
    pl.loop(2, 3)(eliminate)
    gcopy.wait_recv()
    gp64[...] = gps[zh] + gpa[...]
    gp_hi, gp_lo = split(gp64[...])
    for h in range(2):
        cols = pl.ds(pl.multiple_of((zh if h == 0 else 1 - zh) * 256, 256), 256)
        gyp[:, :, :, cols] = dot3(gp_hi, gp_lo, xc_hi[h], xc_lo[h]).reshape(2, 4, 8, 256)
    copy = links.push(gyp.at[1 - k], gyd, me.sib())
    copy.wait_recv()
    gya[...] = gyp[k] + gyd[...]
    cs = [links.push(gya.at[(y + d) % 4], gyy.at[d - 1], me.yd(d)) for d in (1, 2, 3)]
    yg.finish()
    out = pltpu.make_async_copy(ybuf, yr_hbm, lsem.at[1])
    out.start()
    pl.loop(3, 4)(eliminate)
    for copy in cs:
        copy.wait_recv()
    gyb[...] = gya[y] + gyy[0] + (gyy[1] + gyy[2])
    cs = [links.push(gyb, gyz.at[d - 1], me.zd(d)) for d in (1, 2, 3)]
    ycg.finish()
    for copy in cs:
        copy.wait_recv()
    gyo[k, y] = gyb[...] + gyz[0] + (gyz[1] + gyz[2])
    cs = [links.push(gyo.at[k, y], gyo.at[k, y], me.yd(d)) for d in (1, 2, 3)]
    s_hi, s_lo = split(amat[...])

    @pl.loop(0, 2)
    def _(i):
        b_hi, b_lo = split(ycb[pl.ds(i * 4, 4)].reshape(288, 512))
        wt_ref[pl.ds(pl.multiple_of(i * 288, 288), 288), :] = dot3(b_hi, b_lo, s_hi, s_lo)

    for copy in cs:
        copy.wait_recv()
    ycopy = links.push(gyo.at[k], gyo.at[k], me.sib())
    ycopy.wait_recv()
    gy_hi, gy_lo = split(gyo[...].reshape(64, 512))
    w_hi, w_lo = split(wt_ref[...])
    proj_ref[...] = gp64[...] - dot3(gy_hi, gy_lo, w_hi, w_lo, NT)
    out.wait()
    links.finish()


def mega_call(projector, saved, grad):
    vm = lambda *shape, dtype=F32: pltpu.VMEM(shape, dtype)
    scratch = [
        vm(576, 2304), vm(2304, 576, dtype=BF16), vm(2304, 576, dtype=BF16),
        vm(8, 288, 128), vm(8, 72, 128), vm(2, 576, 256, dtype=BF16), vm(2, 576, 256, dtype=BF16),
        vm(4, 4, 2, 16, 2304), vm(2, 4, 4, 2, 72, 256), vm(2, 4, 4, 72, 256), vm(2, 4, 4, 72, 256),
        vm(2, 2, 2, 72, 256), vm(2, 2, 4, 72, 256), vm(2, 3, 72, 256),
        vm(4, 4, 2, 72, 512), vm(8, 72, 512), vm(72, 512),
        vm(2, 4, 4, 8, 640), vm(4, 4, 8, 640), vm(4, 4, 8, 640), vm(3, 4, 8, 640),
        vm(4, 8, 640), vm(3, 8, 640), vm(2, 8, 640), vm(4, 8, 640), vm(2, 4, 4, 8, 640), vm(512, 512),
        vm(4, 2, 64, 576), vm(3, 2, 64, 576), vm(2, 64, 576), vm(64, 576), vm(64, 576),
        vm(2, 4, 8, 512), vm(4, 8, 512), vm(4, 8, 512), vm(3, 8, 512), vm(8, 512), vm(3, 8, 512), vm(2, 4, 8, 512),
        pltpu.SemaphoreType.DMA((NSEM,)), pltpu.SemaphoreType.DMA((NSEM,)), pltpu.SemaphoreType.DMA((2,)),
    ]
    anyspace = pl.BlockSpec(memory_space=pl.ANY)
    vmem = pl.BlockSpec(memory_space=pltpu.VMEM)
    return pl.pallas_call(
        mega,
        out_shape=[
            jax.ShapeDtypeStruct((4, 4, 2, 72, 512), F32),
            jax.ShapeDtypeStruct((576, 512), F32),
            jax.ShapeDtypeStruct((64, 576), F32),
        ],
        in_specs=[anyspace, vmem, vmem],
        out_specs=[anyspace, vmem, vmem],
        scratch_shapes=scratch,
        compiler_params=pltpu.CompilerParams(
            collective_id=0, has_side_effects=True, vmem_limit_bytes=58 * 1024 * 1024),
        name="solve",
    )(projector, saved, grad)


def update_kernel(p_ref, y_ref, wt_ref, o_ref, w):
    @pl.when(pl.program_id(0) == 0)
    def _():
        w_hi, w_lo = split(wt_ref[...])
        w[...] = jnp.concatenate([w_hi, w_hi, w_lo], axis=1)

    y_hi, y_lo = split(y_ref[...])
    y = jnp.concatenate([y_hi, y_lo, y_hi], axis=1)
    o_ref[...] = p_ref[...] - lax.dot_general(w[...], y, NT, preferred_element_type=F32)


def update_call(projector, y_rows, wt):
    block = 768
    return pl.pallas_call(
        update_kernel,
        grid=(2304 // block,),
        out_shape=jax.ShapeDtypeStruct((576, 2304), F32),
        in_specs=[
            pl.BlockSpec((576, block), lambda i: (0, i)),
            pl.BlockSpec((block, 512), lambda i: (i, 0)),
            pl.BlockSpec((576, 512), lambda i: (0, 0)),
        ],
        out_specs=pl.BlockSpec((576, block), lambda i: (0, i)),
        scratch_shapes=[pltpu.VMEM((576, 1536), BF16)],
        compiler_params=pltpu.CompilerParams(vmem_limit_bytes=58 * 1024 * 1024),
        name="update",
    )(projector, y_rows, wt)


def local(projector, saved, grad_slab):
    turned = projector.T
    y_rows, wt, projected = mega_call(turned, saved.T, grad_slab)
    updated = update_call(turned, y_rows.reshape(2304, 512), wt)
    return (updated.T, projected)


def solution(mesh):
    return jax.shard_map(
        local,
        mesh=mesh,
        in_specs=(P("row", "col"), P("col", "row"), P("col", "row")),
        out_specs=(P("row", "col"), P("row", "col")),
        check_vma=False,
    )
```
